256 devices in a mesh: rep: 8 (over y, x_lo), shard: 32 (over z, x_hi, core).
Axes of the slice: x: 4 (x_hi: 2, x_lo: 2; x = x_hi * 2 + x_lo), y: 4, z: 8, core: 2. Of those that a mesh axis runs over, the one named last changes fastest.
Arguments:
- latents: bfloat16 [256, 256, 768], P(('rep', 'shard')), may hold values from -6 to 6
- cotangent: bfloat16 [256, 256, 768], P(('rep', 'shard')), may hold values from -6 to 6
- step_ids: int32 [256], P(('rep', 'shard')), may hold values from 0 to 999
- class_ids: int32 [256], P(('rep', 'shard')), may hold values from 0 to 1000
- class_table: bfloat16 [1001, 768], replicated, may hold values from -6 to 6
- rows_weight: float32 [768, 10752], P('shard'), as said below
- down_weight: float32 [3072, 768], P('shard'), may hold values from -0.109375 to 0.109375
- bias_weight: float32 [11520], P('shard'), may hold values from -0.25 to 0.25
- rows_first: float32 [768, 10752], P('shard'), may hold values from -0.006 to 0.006
- down_first: float32 [3072, 768], P('shard'), may hold values from -0.006 to 0.006
- bias_first: float32 [11520], P('shard'), may hold values from -0.006 to 0.006
- rows_second: float32 [768, 10752], P('shard'), may hold values from 1e-06 to 3e-05
- down_second: float32 [3072, 768], P('shard'), may hold values from 1e-06 to 3e-05
- bias_second: float32 [11520], P('shard'), may hold values from 1e-06 to 3e-05
Outputs:
- output: bfloat16 [256, 256, 768], P(('rep', 'shard'))
- grad_latents: float32 [256, 256, 768], P(('rep', 'shard'))
- grad_rows: float32 [768, 10752], P('shard')
- grad_down: float32 [3072, 768], P('shard')
- grad_bias: float32 [11520], P('shard')
- new_rows: float32 [768, 10752], P('shard')
- new_down: float32 [3072, 768], P('shard')
- new_bias: float32 [11520], P('shard')
- first_rows: float32 [768, 10752], P('shard')
- first_down: float32 [3072, 768], P('shard')
- first_bias: float32 [11520], P('shard')
- second_rows: float32 [768, 10752], P('shard')
- second_down: float32 [3072, 768], P('shard')
- second_bias: float32 [11520], P('shard')
The draws below stay inside these ranges and needn't reach their ends.
Inputs may be any that keep to these rules, and one draw needn't show every extreme that they name: `rows_weight`: independent entries of standard deviation 1 / sqrt(768), except the value block of the qkv matrix (columns 6144 to 6911), whose deviation is 0.3 * sqrt(256) / sqrt(768).
All inputs are finite; a program needn't handle non-finite values.
Results may differ from the reference program's by a relative error of at most 0.028.
Values may be sent and summed in bfloat16 or wider, within the bound.
No kernel may reach another device: no remote copies, remote signals or barrier semaphores. Data moves between devices by JAX's collectives and lax.ppermute only.
A program may use at most 128 MiB of HBM per device.

```python
import math
import jax
import jax.numpy as jnp
from jax import lax

WIDTH = 768
HEAD_FEATURES = 64
MLP_DIM = 3072
CLASSES = 1001
TIMESTEPS = 1000
SEQ_LEN = 256
SEQS = 256
PACK_COLS = 10752
BIAS_LEN = 11520


def draw_rows_weight(key, part):
    columns_all = 10 * WIDTH + MLP_DIM
    column = jnp.arange(columns_all)
    factor = jnp.where((column >= 8 * WIDTH) & (column < 9 * WIDTH), 0.3 * math.sqrt(SEQ_LEN), 1.0) / math.sqrt(WIDTH)
    standard = jnp.clip(jax.random.normal(key, (WIDTH, columns_all), jnp.float32), -6.0, 6.0)
    return standard * factor[None, :].astype(jnp.float32)


def with_ends(drawn, stream_key, least, high):
    extent = drawn.shape
    index_at = [jax.random.randint(jax.random.fold_in(stream_key, axis), (), 0, extent[axis]) for axis in range(len(extent))]
    drawn = drawn.at[tuple(index_at)].set(least)
    longest = extent.index(max(extent))
    index_at[longest] = (index_at[longest] + 1) % extent[longest]
    return drawn.at[tuple(index_at)].set(high)


def shard_levels(stream_key, shape, cuts, low, top_value):
    def one(dim, blocks):
        heights = jax.random.uniform(jax.random.fold_in(jax.random.fold_in(stream_key, 6), dim), (blocks,), jnp.float32, low / len(cuts), top_value / len(cuts))
        return jnp.repeat(jnp.exp(heights), shape[dim] // blocks).reshape((-1,) + (1,) * (len(shape) - dim - 1))

    factor_of = one(*cuts[0])
    for cut in cuts[1:]:
        factor_of = factor_of * one(*cut)
    return factor_of


def bell_draw(rng, dims, deviation, bound, split=(), kind=jnp.bfloat16):
    gain = shard_levels(rng, dims, split, -0.22, 0.18) if split else 1.0
    values = jax.random.normal(rng, dims, jnp.float32) * deviation * gain
    return jnp.minimum(jnp.maximum(values, -bound), bound).astype(kind)


def setup_inputs(seed: int = 0) -> dict:
    seeds = jax.random.split(jax.random.key(seed), 15)
    latents = bell_draw(seeds[0], (SEQS, SEQ_LEN, WIDTH), 1.0, 6.0, ((0, 256),))
    cotangent = bell_draw(seeds[1], (SEQS, SEQ_LEN, WIDTH), 1.0, 6.0, ((0, 256),))
    step_ids = with_ends(jax.random.randint(seeds[2], (SEQS,), 0, TIMESTEPS), jax.random.fold_in(seeds[2], 1), 0, TIMESTEPS - 1).astype(jnp.int32)
    class_ids = with_ends(jax.random.randint(seeds[3], (SEQS,), 0, CLASSES), jax.random.fold_in(seeds[3], 1), 0, CLASSES - 1).astype(jnp.int32)
    class_table = bell_draw(seeds[4], (CLASSES, WIDTH), 1.0, 6.0)
    rows_weight = draw_rows_weight(jax.random.fold_in(seeds[14], 71), 0)
    down_weight = bell_draw(seeds[6], (MLP_DIM, WIDTH), MLP_DIM ** -0.5, 0.109375, ((0, 32),), jnp.float32)
    bias_weight = bell_draw(seeds[7], (BIAS_LEN,), 0.1, 0.25, ((0, 32),), jnp.float32)
    rows_first = bell_draw(seeds[8], (WIDTH, PACK_COLS), 0.001, 0.006, ((0, 32),), jnp.float32)
    down_first = bell_draw(seeds[9], (MLP_DIM, WIDTH), 0.001, 0.006, ((0, 32),), jnp.float32)
    bias_first = bell_draw(seeds[10], (BIAS_LEN,), 0.001, 0.006, ((0, 32),), jnp.float32)
    rows_second = jnp.clip(jnp.exp(math.log(2.9999999242136255e-05) - 3.4011974 * jax.random.uniform(seeds[11], (WIDTH, PACK_COLS), jnp.float32) ** shard_levels(seeds[11], (WIDTH, PACK_COLS), ((0, 32),), -0.2, 0.2)), 9.999999974752427e-07, 2.9999999242136255e-05)
    down_second = jnp.clip(jnp.exp(math.log(2.9999999242136255e-05) - 3.4011974 * jax.random.uniform(seeds[12], (MLP_DIM, WIDTH), jnp.float32) ** shard_levels(seeds[12], (MLP_DIM, WIDTH), ((0, 32),), -0.2, 0.2)), 9.999999974752427e-07, 2.9999999242136255e-05)
    bias_second = jnp.clip(jnp.exp(math.log(2.9999999242136255e-05) - 3.4011974 * jax.random.uniform(seeds[13], (BIAS_LEN,), jnp.float32) ** shard_levels(seeds[13], (BIAS_LEN,), ((0, 32),), -0.2, 0.2)), 9.999999974752427e-07, 2.9999999242136255e-05)
    return {"latents": latents, "cotangent": cotangent, "step_ids": step_ids, "class_ids": class_ids, "class_table": class_table, "rows_weight": rows_weight, "down_weight": down_weight, "bias_weight": bias_weight, "rows_first": rows_first, "down_first": down_first, "bias_first": bias_first, "rows_second": rows_second, "down_second": down_second, "bias_second": bias_second}


norm_eps = 1e-06
gelu_coef = math.sqrt(2.0 / math.pi)
learn_rate = 0.05
beta_one = 0.9
beta_two = 0.95
adam_eps = 1e-08
decay_rate = 0.1
correct_one = 1.0 - 0.9 ** 3
correct_two = 1.0 - 0.95 ** 3

def matmul_result(pattern, first_op, second_op):
    return jnp.einsum(pattern, first_op.astype(jnp.float32), second_op.astype(jnp.float32))

def condition(step_ids, class_ids, class_table):
    half_width = class_table.shape[1] // 2
    frequency = jnp.exp(-math.log(10000.0) * jnp.arange(half_width).astype(jnp.float32) / half_width)
    angles = step_ids.astype(jnp.float32)[:, None] * frequency[None, :]
    time_embed = jnp.concatenate([jnp.cos(angles), jnp.sin(angles)], axis=1)
    label_rows = jnp.take(class_table, class_ids, axis=0).astype(jnp.float32)
    return jax.nn.silu(time_embed + label_rows).astype(jnp.bfloat16)

def normalize(values):
    centred = values - lax.optimization_barrier(jnp.mean(values, axis=-1, keepdims=True))
    recip = lax.rsqrt(lax.optimization_barrier(jnp.mean(centred * centred, axis=-1, keepdims=True)) + norm_eps)
    return (centred * recip, recip)

def norm_back(grad_normed, normed, recip):
    return recip * (grad_normed - lax.optimization_barrier(jnp.mean(grad_normed, axis=-1, keepdims=True)) - normed * lax.optimization_barrier(jnp.mean(grad_normed * normed, axis=-1, keepdims=True)))

def gelu_pair(preactivation):
    tanh_value = jnp.tanh(gelu_coef * (preactivation + 0.044715 * preactivation * preactivation * preactivation))
    result = 0.5 * preactivation * (1.0 + tanh_value)
    slopes = 0.5 * (1.0 + tanh_value) + 0.5 * preactivation * (1.0 - tanh_value * tanh_value) * gelu_coef * (1.0 + 3.0 * 0.044715 * preactivation * preactivation)
    return (result, slopes)

def split_weights(weights):
    rows_mat, lower_weight, bias_vec = weights
    model_width = rows_mat.shape[0]
    hidden_units = lower_weight.shape[0]
    bias_wide = bias_vec.astype(jnp.float32)
    matrices = (rows_mat[:, :6 * model_width], rows_mat[:, 6 * model_width:9 * model_width], rows_mat[:, 9 * model_width:10 * model_width], rows_mat[:, 10 * model_width:], lower_weight)
    biases = (bias_wide[:6 * model_width], bias_wide[6 * model_width:9 * model_width], bias_wide[9 * model_width:10 * model_width], bias_wide[10 * model_width:10 * model_width + hidden_units], bias_wide[10 * model_width + hidden_units:])
    return (matrices, biases)

def score_rows(queries, key_rows):
    return matmul_result('sqhd,skhd->shqk', queries, key_rows) * (1.0 / math.sqrt(HEAD_FEATURES))

def forward(latents, cond_act, weights):
    matrices, biases = split_weights(weights)
    ada_weight, query_key_value_weight, projection_weight, expand_weight, lower_weight = matrices
    ada_bias, query_key_value_bias, projection_bias, expand_bias, lower_bias = biases
    sequence_batch, sequence_length, model_width = latents.shape
    number_heads = model_width // HEAD_FEATURES
    modulation = (jnp.dot(cond_act, ada_weight, preferred_element_type=jnp.float32) + ada_bias).reshape(sequence_batch, 6, 1, model_width)
    shift_one, scale_one, gate_one, shift_two, scale_two, gate_two = [modulation[:, position] for position in range(6)]
    residual = latents.astype(jnp.float32)
    normed_one, recip_one = normalize(residual)
    first_input = (normed_one * (1.0 + scale_one) + shift_one).astype(jnp.bfloat16)
    projection_rows = matmul_result('ajx,xo->ajo', first_input, query_key_value_weight) + query_key_value_bias
    projection_rows = projection_rows.astype(jnp.bfloat16).reshape(sequence_batch, sequence_length, 3, number_heads, HEAD_FEATURES)
    queries, key_rows, values = (projection_rows[:, :, 0], projection_rows[:, :, 1], projection_rows[:, :, 2])
    scores = score_rows(queries, key_rows)
    row_max = lax.optimization_barrier(jnp.max(scores, axis=-1, keepdims=True))
    log_total = row_max + jnp.log(lax.optimization_barrier(jnp.sum(jnp.exp(scores - row_max), axis=-1, keepdims=True)))
    attend = jnp.exp(scores - log_total).astype(jnp.bfloat16)
    blend_rows = matmul_result('shqk,skhd->sqhd', attend, values).astype(jnp.bfloat16).reshape(sequence_batch, sequence_length, model_width)
    attention_output = matmul_result('ajx,xo->ajo', blend_rows, projection_weight) + projection_bias
    residual_two = residual + gate_one * attention_output
    normed_two, recip_two = normalize(residual_two)
    second_input = (normed_two * (1.0 + scale_two) + shift_two).astype(jnp.bfloat16)
    preactivation = matmul_result('xyz,zw->xyw', second_input, expand_weight) + expand_bias
    gelu_value, slopes = gelu_pair(preactivation)
    activated_rows = gelu_value.astype(jnp.bfloat16)
    perceptron_output = matmul_result('khw,we->khe', activated_rows, lower_weight) + lower_bias
    output = (residual_two + gate_two * perceptron_output).astype(jnp.bfloat16)
    stored = (modulation, normed_one, recip_one, first_input, queries, key_rows, values, log_total, blend_rows, attention_output, normed_two, recip_two, second_input, slopes, activated_rows, perceptron_output)
    return (output, stored)

def backward(cotangent, cond_act, weights, stored):
    matrices, biases = split_weights(weights)
    ada_weight, query_key_value_weight, projection_weight, expand_weight, lower_weight = matrices
    modulation, normed_one, recip_one, first_input, queries, key_rows, values, log_total, blend_rows, attention_output, normed_two, recip_two, second_input, slopes, activated_rows, perceptron_output = stored
    sequence_batch, sequence_length, model_width = cotangent.shape
    number_heads = model_width // HEAD_FEATURES
    shift_one, scale_one, gate_one, shift_two, scale_two, gate_two = [modulation[:, position] for position in range(6)]
    grad_out = cotangent.astype(jnp.float32)
    grad_gate_two = lax.optimization_barrier(jnp.sum(grad_out * perceptron_output, axis=1))
    perceptron_gradient = (grad_out * gate_two).astype(jnp.bfloat16)
    activated_gradient = matmul_result('abj,qj->abq', perceptron_gradient, lower_weight)
    preactivation_gradient = (activated_gradient * slopes).astype(jnp.bfloat16)
    second_input_gradient = matmul_result('wkr,ar->wka', preactivation_gradient, expand_weight)
    grad_shift_two = lax.optimization_barrier(jnp.sum(second_input_gradient, axis=1))
    grad_scale_two = lax.optimization_barrier(jnp.sum(second_input_gradient * normed_two, axis=1))
    grad_residual = grad_out + norm_back(second_input_gradient * (1.0 + scale_two), normed_two, recip_two)
    grad_gate_one = lax.optimization_barrier(jnp.sum(grad_residual * attention_output, axis=1))
    attention_output_gradient = (grad_residual * gate_one).astype(jnp.bfloat16)
    blend_gradient = matmul_result('rhm,pm->rhp', attention_output_gradient, projection_weight).astype(jnp.bfloat16).reshape(sequence_batch, sequence_length, number_heads, HEAD_FEATURES)
    attend = jnp.exp(score_rows(queries, key_rows) - log_total)
    grad_attend = matmul_result('sqhd,skhd->shqk', blend_gradient, values)
    row_delta = lax.optimization_barrier(jnp.sum(attend * grad_attend, axis=-1, keepdims=True))
    grad_scores = (attend * (grad_attend - row_delta) * (1.0 / math.sqrt(HEAD_FEATURES))).astype(jnp.bfloat16)
    grad_queries = matmul_result('shqk,skhd->sqhd', grad_scores, key_rows)
    grad_keys = matmul_result('shqk,sqhd->skhd', grad_scores, queries)
    grad_values = matmul_result('shqk,sqhd->skhd', attend.astype(jnp.bfloat16), blend_gradient)
    projection_gradient = jnp.stack([grad_queries, grad_keys, grad_values], axis=2).astype(jnp.bfloat16).reshape(sequence_batch, sequence_length, 3 * model_width)
    first_input_gradient = matmul_result('rhm,pm->rhp', projection_gradient, query_key_value_weight)
    grad_shift_one = lax.optimization_barrier(jnp.sum(first_input_gradient, axis=1))
    grad_scale_one = lax.optimization_barrier(jnp.sum(first_input_gradient * normed_one, axis=1))
    grad_latents = grad_residual + norm_back(first_input_gradient * (1.0 + scale_one), normed_one, recip_one)
    grad_modulation = jnp.stack([grad_shift_one, grad_scale_one, grad_gate_one, grad_shift_two, grad_scale_two, grad_gate_two], axis=1).reshape(sequence_batch, 6 * model_width).astype(jnp.bfloat16)
    tokens = sequence_batch * sequence_length
    sources = (cond_act, first_input.reshape(tokens, model_width), blend_rows.reshape(tokens, model_width), second_input.reshape(tokens, model_width))
    targets = (grad_modulation, projection_gradient.reshape(tokens, 3 * model_width), attention_output_gradient.reshape(tokens, model_width), preactivation_gradient.reshape(tokens, -1))
    mlp_rows = perceptron_gradient.reshape(tokens, model_width)
    bias_term = jnp.concatenate([lax.optimization_barrier(jnp.sum(target.astype(jnp.float32), axis=0)) for target in targets] + [lax.optimization_barrier(jnp.sum(mlp_rows.astype(jnp.float32), axis=0))])
    down_pair = (activated_rows.reshape(tokens, -1), mlp_rows)
    return (grad_latents, sources, targets, down_pair, bias_term)

def keep_all(source):
    return source

def rows_term(sources, targets, selector):
    pieces = [jnp.dot(selector(source).T, target, preferred_element_type=jnp.float32) for source, target in zip(sources, targets)]
    return jnp.concatenate(pieces, axis=1)

def adamw(weight, first_mom, second_mom, gradient, decay):
    new_first = beta_one * first_mom + (1.0 - beta_one) * gradient
    new_second = beta_two * second_mom + (1.0 - beta_two) * gradient * gradient
    update = new_first / correct_one / (jnp.sqrt(new_second / correct_two) + adam_eps)
    return (weight - learn_rate * (update + decay * weight), new_first, new_second)

def reference(latents, cotangent, step_ids, class_ids, class_table, rows_weight, down_weight, bias_weight, rows_first, down_first, bias_first, rows_second, down_second, bias_second):
    weights = (rows_weight.astype(jnp.bfloat16), down_weight.astype(jnp.bfloat16), bias_weight.astype(jnp.bfloat16))

    def one_sequence(totals, sample):
        latent_row, cotan_row, step_row, class_row = sample
        cond_act = condition(step_row[None], class_row[None], class_table)
        output, stored = forward(latent_row[None], cond_act, weights)
        grad_latents, sources, targets, down_pair, bias_term = backward(cotan_row[None], cond_act, weights, stored)
        rows_total, down_total, bias_total = totals
        rows_total = rows_total + rows_term(sources, targets, keep_all)
        down_total = down_total + jnp.dot(down_pair[0].T, down_pair[1], preferred_element_type=jnp.float32)
        return ((rows_total, down_total, bias_total + bias_term), (output[0], grad_latents[0]))
    initial = (jnp.zeros(rows_weight.shape, jnp.float32), jnp.zeros(down_weight.shape, jnp.float32), jnp.zeros(bias_weight.shape, jnp.float32))
    totals, results = lax.scan(one_sequence, initial, (latents, cotangent, step_ids, class_ids))
    factor = 1.0 / (latents.shape[0] * latents.shape[1])
    grad_rows = totals[0] * factor
    grad_down = totals[1] * factor
    grad_bias = totals[2] * factor
    new_rows, first_rows, second_rows = adamw(rows_weight, rows_first, rows_second, grad_rows, decay_rate)
    new_down, first_down, second_down = adamw(down_weight, down_first, down_second, grad_down, decay_rate)
    new_bias, first_bias, second_bias = adamw(bias_weight, bias_first, bias_second, grad_bias, 0.0)
    return (results[0], results[1], grad_rows, grad_down, grad_bias, new_rows, new_down, new_bias, first_rows, first_down, first_bias, second_rows, second_down, second_bias)
```

```python
import math

import jax
import jax.numpy as jnp
from jax import lax
from jax.sharding import PartitionSpec as P

HEAD_FEATURES = 64


norm_eps = 1e-06
gelu_coef = math.sqrt(2.0 / math.pi)
learn_rate = 0.05
beta_one = 0.9
beta_two = 0.95
adam_eps = 1e-08
decay_rate = 0.1
correct_one = 1.0 - 0.9**3
correct_two = 1.0 - 0.95**3


def matmul_result(pattern, first_op, second_op):
    return jnp.einsum(pattern, first_op, second_op, preferred_element_type=jnp.float32)


def normalize(values):
    centred = values - jnp.mean(values, axis=-1, keepdims=True)
    recip = lax.rsqrt(jnp.mean(centred * centred, axis=-1, keepdims=True) + norm_eps)
    return (centred * recip, recip)


def norm_back(grad_normed, normed, recip):
    return recip * (
        grad_normed
        - jnp.mean(grad_normed, axis=-1, keepdims=True)
        - normed * jnp.mean(grad_normed * normed, axis=-1, keepdims=True)
    )


def gelu_pair(preactivation):
    tanh_value = jnp.tanh(
        gelu_coef * (preactivation + 0.044715 * preactivation * preactivation * preactivation)
    )
    result = 0.5 * preactivation * (1.0 + tanh_value)
    slopes = 0.5 * (1.0 + tanh_value) + 0.5 * preactivation * (
        1.0 - tanh_value * tanh_value
    ) * gelu_coef * (1.0 + 3.0 * 0.044715 * preactivation * preactivation)
    return (result, slopes)


def score_rows(queries, key_rows):
    return matmul_result("sqhd,skhd->shqk", queries, key_rows) * (1.0 / math.sqrt(HEAD_FEATURES))


def forward(latents, modulation, matrices, biases):
    query_key_value_weight, projection_weight, expand_weight, lower_weight = matrices
    query_key_value_bias, projection_bias, expand_bias, lower_bias = biases
    sequence_batch, sequence_length, model_width = latents.shape
    number_heads = model_width // HEAD_FEATURES
    modulation = modulation.reshape(sequence_batch, 6, 1, model_width)
    shift_one, scale_one, gate_one, shift_two, scale_two, gate_two = [
        modulation[:, position] for position in range(6)
    ]
    residual = latents.astype(jnp.float32)
    normed_one, recip_one = normalize(residual)
    first_input = (normed_one * (1.0 + scale_one) + shift_one).astype(jnp.bfloat16)
    projection_rows = (
        matmul_result("ajx,xo->ajo", first_input, query_key_value_weight) + query_key_value_bias
    )
    projection_rows = projection_rows.astype(jnp.bfloat16).reshape(
        sequence_batch, sequence_length, 3, number_heads, HEAD_FEATURES
    )
    queries, key_rows, values = (
        projection_rows[:, :, 0],
        projection_rows[:, :, 1],
        projection_rows[:, :, 2],
    )
    scores = score_rows(queries, key_rows)
    row_max = jnp.max(scores, axis=-1, keepdims=True)
    log_total = row_max + jnp.log(jnp.sum(jnp.exp(scores - row_max), axis=-1, keepdims=True))
    attend = jnp.exp(scores - log_total).astype(jnp.bfloat16)
    blend_rows = (
        matmul_result("shqk,skhd->sqhd", attend, values)
        .astype(jnp.bfloat16)
        .reshape(sequence_batch, sequence_length, model_width)
    )
    attention_output = matmul_result("ajx,xo->ajo", blend_rows, projection_weight) + projection_bias
    residual_two = residual + gate_one * attention_output
    normed_two, recip_two = normalize(residual_two)
    second_input = (normed_two * (1.0 + scale_two) + shift_two).astype(jnp.bfloat16)
    preactivation = matmul_result("xyz,zw->xyw", second_input, expand_weight) + expand_bias
    gelu_value, slopes = gelu_pair(preactivation)
    activated_rows = gelu_value.astype(jnp.bfloat16)
    perceptron_output = matmul_result("khw,we->khe", activated_rows, lower_weight) + lower_bias
    output = (residual_two + gate_two * perceptron_output).astype(jnp.bfloat16)
    stored = (
        modulation,
        normed_one,
        recip_one,
        first_input,
        queries,
        key_rows,
        values,
        log_total,
        blend_rows,
        attention_output,
        normed_two,
        recip_two,
        second_input,
        slopes,
        activated_rows,
        perceptron_output,
    )
    return (output, stored)


def backward(cotangent, matrices, stored):
    query_key_value_weight, projection_weight, expand_weight, lower_weight = matrices
    (
        modulation,
        normed_one,
        recip_one,
        first_input,
        queries,
        key_rows,
        values,
        log_total,
        blend_rows,
        attention_output,
        normed_two,
        recip_two,
        second_input,
        slopes,
        activated_rows,
        perceptron_output,
    ) = stored
    sequence_batch, sequence_length, model_width = cotangent.shape
    number_heads = model_width // HEAD_FEATURES
    shift_one, scale_one, gate_one, shift_two, scale_two, gate_two = [
        modulation[:, position] for position in range(6)
    ]
    grad_out = cotangent.astype(jnp.float32)
    grad_gate_two = jnp.sum(grad_out * perceptron_output, axis=1)
    perceptron_gradient = (grad_out * gate_two).astype(jnp.bfloat16)
    activated_gradient = matmul_result("abj,qj->abq", perceptron_gradient, lower_weight)
    preactivation_gradient = (activated_gradient * slopes).astype(jnp.bfloat16)
    second_input_gradient = matmul_result("wkr,ar->wka", preactivation_gradient, expand_weight)
    grad_shift_two = jnp.sum(second_input_gradient, axis=1)
    grad_scale_two = jnp.sum(second_input_gradient * normed_two, axis=1)
    grad_residual = grad_out + norm_back(
        second_input_gradient * (1.0 + scale_two), normed_two, recip_two
    )
    grad_gate_one = jnp.sum(grad_residual * attention_output, axis=1)
    attention_output_gradient = (grad_residual * gate_one).astype(jnp.bfloat16)
    blend_gradient = (
        matmul_result("rhm,pm->rhp", attention_output_gradient, projection_weight)
        .astype(jnp.bfloat16)
        .reshape(sequence_batch, sequence_length, number_heads, HEAD_FEATURES)
    )
    attend = jnp.exp(score_rows(queries, key_rows) - log_total)
    grad_attend = matmul_result("sqhd,skhd->shqk", blend_gradient, values)
    row_delta = jnp.sum(attend * grad_attend, axis=-1, keepdims=True)
    grad_scores = (attend * (grad_attend - row_delta) * (1.0 / math.sqrt(HEAD_FEATURES))).astype(
        jnp.bfloat16
    )
    grad_queries = matmul_result("shqk,skhd->sqhd", grad_scores, key_rows)
    grad_keys = matmul_result("shqk,sqhd->skhd", grad_scores, queries)
    grad_values = matmul_result("shqk,sqhd->skhd", attend.astype(jnp.bfloat16), blend_gradient)
    projection_gradient = (
        jnp.stack([grad_queries, grad_keys, grad_values], axis=2)
        .astype(jnp.bfloat16)
        .reshape(sequence_batch, sequence_length, 3 * model_width)
    )
    first_input_gradient = matmul_result("rhm,pm->rhp", projection_gradient, query_key_value_weight)
    grad_shift_one = jnp.sum(first_input_gradient, axis=1)
    grad_scale_one = jnp.sum(first_input_gradient * normed_one, axis=1)
    grad_latents = grad_residual + norm_back(
        first_input_gradient * (1.0 + scale_one), normed_one, recip_one
    )
    grad_modulation = (
        jnp.stack(
            [
                grad_shift_one,
                grad_scale_one,
                grad_gate_one,
                grad_shift_two,
                grad_scale_two,
                grad_gate_two,
            ],
            axis=1,
        )
        .reshape(sequence_batch, 6 * model_width)
        .astype(jnp.bfloat16)
    )
    tokens = sequence_batch * sequence_length
    sources = (
        first_input.reshape(tokens, model_width),
        blend_rows.reshape(tokens, model_width),
        second_input.reshape(tokens, model_width),
    )
    targets = (
        projection_gradient.reshape(tokens, 3 * model_width),
        attention_output_gradient.reshape(tokens, model_width),
        preactivation_gradient.reshape(tokens, -1),
    )
    mlp_rows = perceptron_gradient.reshape(tokens, model_width)
    bias_term = jnp.concatenate(
        [grad_modulation.reshape(-1).astype(jnp.float32)]
        + [jnp.sum(target.astype(jnp.float32), axis=0) for target in targets]
        + [jnp.sum(mlp_rows.astype(jnp.float32), axis=0)]
    )
    down_pair = (activated_rows.reshape(tokens, -1), mlp_rows)
    return (grad_latents, sources, targets, down_pair, bias_term)


def adamw(weight, first_mom, second_mom, gradient, decay):
    new_first = beta_one * first_mom + (1.0 - beta_one) * gradient
    new_second = beta_two * second_mom + (1.0 - beta_two) * gradient * gradient
    update = new_first / correct_one / (jnp.sqrt(new_second / correct_two) + adam_eps)
    return (weight - learn_rate * (update + decay * weight), new_first, new_second)

def place(rep, shard):
    y, xl = rep >> 1, rep & 1
    z, xh, c = shard >> 2, (shard >> 1) & 1, shard & 1
    return {
        "z2": z >> 2,
        "z1": (z >> 1) & 1,
        "z0": z & 1,
        "xh": xh,
        "c": c,
        "g1": y >> 1,
        "g0": (y & 1) ^ (y >> 1),
        "xg": xl ^ xh,
    }


BITS = ("z2", "z1", "z0", "xh", "c", "g1", "g0", "xg")


def index_of(bits):
    z = bits["z2"] * 4 + bits["z1"] * 2 + bits["z0"]
    y = bits["g1"] * 2 + (bits["g1"] ^ bits["g0"])
    xl = bits["xg"] ^ bits["xh"]
    return (y * 2 + xl) * 32 + z * 4 + bits["xh"] * 2 + bits["c"]


def pairs_of(bit):
    pairs = []
    for rep in range(8):
        for shard in range(32):
            bits = place(rep, shard)
            there = dict(bits)
            there[bit] ^= 1
            pairs.append((index_of(bits), index_of(there)))
    return pairs


PAIRS = {bit: pairs_of(bit) for bit in BITS}


def swap(values, bit):
    return lax.ppermute(values, ("rep", "shard"), PAIRS[bit])


def join(mine, theirs, here, axis):
    low = jnp.where(here == 0, mine, theirs)
    high = jnp.where(here == 0, theirs, mine)
    return jnp.concatenate([low, high], axis=axis)


def gather(values, bit, here, axis):
    return join(values, swap(values, bit), here[bit], axis)


def take_half(values, which, axis):
    half = values.shape[axis] // 2
    parts = values.reshape(values.shape[:axis] + (2, half) + values.shape[axis + 1 :])
    return lax.dynamic_index_in_dim(parts, which, axis, keepdims=False)


def add_up(first, second):
    return (first.astype(jnp.float32) + second.astype(jnp.float32)).astype(first.dtype)


def scatter(values, bit, here, axis):
    sent = take_half(values, 1 - here[bit], axis)
    kept = take_half(values, here[bit], axis)
    return add_up(kept, swap(sent, bit))


STREAMS = (
    ("xh", "xg", "g0", "g1"),
    ("xg", "xh", "g1", "g0"),
    ("g0", "g1", "xh", "xg"),
    ("g1", "g0", "xg", "xh"),
)
AXIS = {"g1": 0, "g0": 1, "xg": 2, "xh": 3}
SHARD_BITS = ("z2", "z1", "z0", "xh", "c")
BLOCK = 24
PIECE = 384


def gather_weights(rows_weight, down_weight, here):
    piece = here["g1"] * 4 + here["g0"] * 2 + here["xg"]
    down_rows = BLOCK * (here["g1"] * 2 + here["g0"])
    mine = jnp.stack(
        [
            lax.dynamic_slice(rows_weight, (0, 4608 + PIECE * piece), (BLOCK, PIECE)),
            lax.dynamic_slice(rows_weight, (0, 7680 + PIECE * piece), (BLOCK, PIECE)),
            lax.dynamic_slice(down_weight, (down_rows, PIECE * here["xg"]), (BLOCK, PIECE)),
        ]
    ).astype(jnp.bfloat16)
    values = mine.reshape(1, 1, 1, 3, BLOCK, PIECE)
    for axis, bit in ((2, "z0"), (1, "z1"), (0, "z2")):
        values = gather(values, bit, here, axis)
    values = values.reshape(8, 3, BLOCK, PIECE)
    results = []
    for number, order in enumerate(STREAMS):
        part = values[2 * number : 2 * number + 2].reshape(1, 1, 1, 1, 1, 2, 3, BLOCK, PIECE)
        for bit in order[:-1]:
            part = gather(part, bit, here, AXIS[bit])
        last = swap(part, order[-1])
        pieces = []
        for half in (part, last):
            pieces.append(gather(half, "c", here, 4))
        results.append(join(pieces[0], pieces[1], here[order[-1]], AXIS[order[-1]]))
    return results


def unpack(results):
    whole = []
    for number in range(2):
        block = jnp.concatenate(
            [
                result[:, :, :, :, :, :, number].transpose(0, 1, 2, 5, 3, 4, 6, 7).reshape(8, 192, PIECE)
                for result in results
            ],
            axis=1,
        )
        whole.append(jnp.concatenate([block[piece] for piece in range(8)], axis=1))
    down = jnp.concatenate(
        [
            result[:, :, :, :, :, :, 2].transpose(2, 5, 3, 4, 0, 1, 6, 7).reshape(2, 768, PIECE)
            for result in results
        ],
        axis=1,
    )
    down = jnp.concatenate([down[0], down[1]], axis=1)
    return whole[0][:, :2304], whole[0][:, 2304:], whole[1], down


def rows_pieces(gradient):
    pieces = jnp.stack([gradient[:, PIECE * k : PIECE * (k + 1)] for k in range(8)])
    return pieces.reshape(2, 2, 2, 1, 8, 2, 2, BLOCK, PIECE)


def down_pieces(gradient):
    pieces = jnp.stack([gradient[:, :PIECE], gradient[:, PIECE:]])
    pieces = pieces.reshape(2, 1, 8, 2, 2, 2, 2, BLOCK, PIECE)
    return pieces.transpose(5, 6, 0, 1, 2, 3, 4, 7, 8)


def scatter_group(parts, here):
    halves = [scatter(part, "c", here, 6).reshape(2, 2, 2, 8, 2, BLOCK, PIECE) for part in parts]
    results = []
    for number, order in enumerate(STREAMS):
        cur = jnp.stack([half[:, :, :, 2 * number : 2 * number + 2] for half in halves])
        cur = cur.transpose(1, 2, 3, 5, 0, 4, 6, 7)
        for bit in order:
            cur = scatter(cur, bit, here, AXIS[bit])
        results.append(cur.reshape(len(parts), 2, BLOCK, PIECE))
    return jnp.concatenate(results, axis=1)


def scatter_z(values, here):
    for bit in ("z2", "z1", "z0"):
        values = scatter(values, bit, here, 1)
    return values[:, 0]


def gather_pieces(values, here):
    number = values.shape[0]
    values = values.reshape(1, 1, 1, number, BLOCK, PIECE)
    for axis, bit in ((2, "xg"), (1, "g0"), (0, "g1")):
        values = gather(values, bit, here, axis)
    return values.reshape(8, number, BLOCK, PIECE)


def gather_shard(vector, here):
    values = vector.reshape(1, 1, 1, 1, 1, -1)
    for axis, bit in ((4, "c"), (3, "xh"), (2, "z0"), (1, "z1"), (0, "z2")):
        values = gather(values, bit, here, axis)
    return values.reshape(32, -1)


def scatter_shard(values, here):
    width = values.shape[-1]
    cur = values.reshape(2, 2, 2, 2, 2, width)
    for bit, axis in (("c", 4), ("xh", 3), ("z0", 2), ("z1", 1), ("z2", 0)):
        cur = scatter(cur, bit, here, axis)
    return cur.reshape(width)


def condition_columns(steps, classes, class_table, shard):
    half_width = class_table.shape[1] // 2
    column = BLOCK * shard + jnp.arange(BLOCK)
    place_of = jnp.where(column < half_width, column, column - half_width)
    frequency = jnp.exp(-math.log(10000.0) * place_of.astype(jnp.float32) / half_width)
    angles = steps[:, None] * frequency[None, :]
    time_embed = jnp.where(column[None, :] < half_width, jnp.cos(angles), jnp.sin(angles))
    label_rows = jnp.take(class_table, classes, axis=0)
    label_part = lax.dynamic_slice(label_rows, (0, BLOCK * shard), (label_rows.shape[0], BLOCK))
    return jax.nn.silu(time_embed + label_part.astype(jnp.float32)).astype(jnp.bfloat16)


def local(
    latents,
    cotangent,
    step_ids,
    class_ids,
    class_table,
    rows_weight,
    down_weight,
    bias_weight,
    rows_first,
    down_first,
    bias_first,
    rows_second,
    down_second,
    bias_second,
):
    rep, shard = lax.axis_index("rep"), lax.axis_index("shard")
    here = place(rep, shard)
    width = latents.shape[-1]
    bias_here = bias_weight.astype(jnp.bfloat16).astype(jnp.float32)
    small = jnp.concatenate(
        [
            bias_here,
            step_ids.astype(jnp.float32),
            class_ids.astype(jnp.float32),
            jnp.zeros((22,), jnp.float32),
        ]
    )
    small = gather_shard(small, here)
    biases = small[:, :360].reshape(-1)
    classes = small[:, 361].astype(jnp.int32)
    cond_columns = condition_columns(small[:, 360], classes, class_table, shard)
    ada_rows = rows_weight[:, : 6 * width].astype(jnp.bfloat16)
    partial = jnp.dot(cond_columns, ada_rows, preferred_element_type=jnp.float32)
    modulation = scatter_shard(partial, here) + biases[: 6 * width]
    matrices = unpack(gather_weights(rows_weight, down_weight, here))
    bias_parts = (
        biases[6 * width : 9 * width],
        biases[9 * width : 10 * width],
        biases[10 * width : 14 * width],
        biases[14 * width :],
    )
    output, stored = forward(latents, modulation, matrices, bias_parts)
    grad_latents, sources, targets, down_pair, bias_term = backward(cotangent, matrices, stored)
    down_term = jnp.dot(down_pair[0].T, down_pair[1], preferred_element_type=jnp.float32)
    expand_term = jnp.dot(sources[2].T, targets[2], preferred_element_type=jnp.float32)
    first = scatter_group(
        [
            rows_pieces(expand_term.astype(jnp.bfloat16)),
            down_pieces(down_term.astype(jnp.bfloat16)),
        ],
        here,
    )
    attend_terms = jnp.concatenate(
        [
            jnp.dot(sources[0].T, targets[0], preferred_element_type=jnp.float32),
            jnp.dot(sources[1].T, targets[1], preferred_element_type=jnp.float32),
        ],
        axis=1,
    ).astype(jnp.bfloat16)
    second = scatter_group([rows_pieces(attend_terms)], here)
    owned = scatter_z(jnp.concatenate([second, first]), here)
    owned = gather_pieces(owned, here).astype(jnp.float32)
    vectors = gather_shard(bias_term.astype(jnp.bfloat16), here)
    ada_term = lax.dot_general(
        cond_columns,
        vectors[:, : 6 * width],
        (((0,), (0,)), ((), ())),
        preferred_element_type=jnp.float32,
    )
    bias_sum = jnp.sum(vectors.astype(jnp.float32), axis=0)
    bias_sum = lax.dynamic_slice(bias_sum, (360 * shard,), (360,))
    packed = jnp.concatenate(
        [ada_term, jnp.pad(bias_sum, (0, 24)).reshape(3, 128).repeat(8, axis=0)], axis=1
    ).astype(jnp.bfloat16)
    for bit in ("xg", "g0", "g1"):
        packed = add_up(packed, swap(packed, bit))
    packed = packed.astype(jnp.float32)
    factor = 1.0 / 65536
    grad_rows = (
        jnp.concatenate(
            [packed[:, : 6 * width]]
            + [owned[piece, 0] for piece in range(8)]
            + [owned[piece, 1] for piece in range(8)],
            axis=1,
        )
        * factor
    )
    grad_down = (
        jnp.concatenate(
            [
                jnp.concatenate([owned[2 * row, 2], owned[2 * row + 1, 2]], axis=1)
                for row in range(4)
            ],
            axis=0,
        )
        * factor
    )
    grad_bias = packed[::8, 6 * width :].reshape(-1)[:360] * factor
    new_rows, first_rows, second_rows = adamw(
        rows_weight, rows_first, rows_second, grad_rows, decay_rate
    )
    new_down, first_down, second_down = adamw(
        down_weight, down_first, down_second, grad_down, decay_rate
    )
    new_bias, first_bias, second_bias = adamw(bias_weight, bias_first, bias_second, grad_bias, 0.0)
    return (
        output,
        grad_latents,
        grad_rows,
        grad_down,
        grad_bias,
        new_rows,
        new_down,
        new_bias,
        first_rows,
        first_down,
        first_bias,
        second_rows,
        second_down,
        second_bias,
    )


def solution(mesh):
    placed = (
        P(("rep", "shard"), None, None),
        P(("rep", "shard"), None, None),
        P(("rep", "shard")),
        P(("rep", "shard")),
        P(),
        P("shard", None),
        P("shard", None),
        P("shard"),
        P("shard", None),
        P("shard", None),
        P("shard"),
        P("shard", None),
        P("shard", None),
        P("shard"),
    )
    return jax.shard_map(
        local,
        mesh=mesh,
        in_specs=placed,
        out_specs=(
            P(("rep", "shard"), None, None),
            P(("rep", "shard"), None, None),
            P("shard", None),
            P("shard", None),
            P("shard"),
            P("shard", None),
            P("shard", None),
            P("shard"),
            P("shard", None),
            P("shard", None),
            P("shard"),
            P("shard", None),
            P("shard", None),
            P("shard"),
        ),
        check_vma=False,
    )
```

```python
import math

import jax
import jax.numpy as jnp
from jax import lax
from jax.experimental import pallas as pl
from jax.experimental.pallas import tpu as pltpu
from jax.sharding import PartitionSpec as P

HEAD_FEATURES = 64


norm_eps = 1e-06
gelu_coef = math.sqrt(2.0 / math.pi)
learn_rate = 0.05
beta_one = 0.9
beta_two = 0.95
adam_eps = 1e-08
decay_rate = 0.1
correct_one = 1.0 - 0.9**3
correct_two = 1.0 - 0.95**3


def matmul_result(pattern, first_op, second_op):
    return jnp.einsum(pattern, first_op, second_op, preferred_element_type=jnp.float32)


def normalize(values):
    centred = values - jnp.mean(values, axis=-1, keepdims=True)
    recip = lax.rsqrt(jnp.mean(centred * centred, axis=-1, keepdims=True) + norm_eps)
    return (centred * recip, recip)


def norm_back(grad_normed, normed, recip):
    return recip * (
        grad_normed
        - jnp.mean(grad_normed, axis=-1, keepdims=True)
        - normed * jnp.mean(grad_normed * normed, axis=-1, keepdims=True)
    )


def gelu_pair(preactivation):
    tanh_value = jnp.tanh(
        gelu_coef * (preactivation + 0.044715 * preactivation * preactivation * preactivation)
    )
    result = 0.5 * preactivation * (1.0 + tanh_value)
    slopes = 0.5 * (1.0 + tanh_value) + 0.5 * preactivation * (
        1.0 - tanh_value * tanh_value
    ) * gelu_coef * (1.0 + 3.0 * 0.044715 * preactivation * preactivation)
    return (result, slopes)


def dot_of(left, right, left_axis, right_axis):
    return lax.dot_general(
        left,
        right,
        (((left_axis,), (right_axis,)), ((), ())),
        preferred_element_type=jnp.float32,
    )


def token_sum(values):
    return jnp.sum(values, axis=0, keepdims=True)


def head_masks():
    lane = lax.broadcasted_iota(jnp.int32, (1, 2 * HEAD_FEATURES), 1)
    return [(lane // HEAD_FEATURES == head).astype(jnp.bfloat16) for head in range(2)]


SCORE_SCALE = 1.0 / math.sqrt(HEAD_FEATURES)


def attention_forward_kernel(
    x_ref, mod_ref, weight_ref, bias_ref, a1_ref, qkv_ref, lse_ref, o_ref, att_ref, x1_ref, a2_ref
):
    x = x_ref[...].astype(jnp.float32)
    normed, _ = normalize(x)
    a1_ref[...] = (normed * (1.0 + mod_ref[1:2, :]) + mod_ref[0:1, :]).astype(jnp.bfloat16)
    for piece in range(6):
        cols = slice(PIECE * piece, PIECE * (piece + 1))
        product = dot_of(a1_ref[...], weight_ref[piece], 1, 0) + bias_ref[piece]
        qkv_ref[:, cols] = product.astype(jnp.bfloat16)
    masks = head_masks()

    def pair(number, carry):
        at_q = pl.ds(pl.multiple_of(number * 128, 128), 128)
        at_k = pl.ds(pl.multiple_of(number * 128 + 768, 128), 128)
        at_v = pl.ds(pl.multiple_of(number * 128 + 1536, 128), 128)
        queries, key_rows, values = qkv_ref[:, at_q], qkv_ref[:, at_k], qkv_ref[:, at_v]
        total = jnp.zeros((256, 128), jnp.float32)
        for head in range(2):
            scores = dot_of(key_rows * masks[head], queries, 1, 1) * SCORE_SCALE
            top = jnp.max(scores, axis=0, keepdims=True)
            lse = top + jnp.log(jnp.sum(jnp.exp(scores - top), axis=0, keepdims=True))
            lse_ref[2 * number + head] = lse
            attend = jnp.exp(scores - lse).astype(jnp.bfloat16)
            total = total + dot_of(attend, values * masks[head], 0, 0)
        o_ref[:, at_q] = total.astype(jnp.bfloat16)
        return carry

    lax.fori_loop(0, 6, pair, 0)
    for half in range(2):
        cols = slice(PIECE * half, PIECE * (half + 1))
        att = dot_of(o_ref[...], weight_ref[6 + half], 1, 0) + bias_ref[6 + half]
        att_ref[:, cols] = att
        x1_ref[:, cols] = x_ref[:, cols].astype(jnp.float32) + mod_ref[2:3, cols] * att
    normed, _ = normalize(x1_ref[...])
    a2_ref[...] = (normed * (1.0 + mod_ref[4:5, :]) + mod_ref[3:4, :]).astype(jnp.bfloat16)


def perceptron_kernel(
    a2_ref,
    x1_ref,
    att_ref,
    dy_ref,
    mod_ref,
    expand_ref,
    lower_ref,
    bias_ref,
    lower_bias_ref,
    out_ref,
    dx1_ref,
    datt_ref,
    expand_grad_ref,
    lower_grad_ref,
    hidden_sum_ref,
    sums_ref,
    g_ref,
    slope_ref,
    dm_ref,
    total_ref,
):
    total_ref[...] = jnp.zeros_like(total_ref)

    def rise(piece, carry):
        hidden = dot_of(a2_ref[...], expand_ref[piece], 1, 0) + bias_ref[piece]
        value, slope = gelu_pair(hidden)
        value = value.astype(jnp.bfloat16)
        g_ref[piece] = value
        slope_ref[piece] = slope
        rows = pl.ds(pl.multiple_of(piece * PIECE, PIECE), PIECE)
        for half in range(2):
            cols = slice(PIECE * half, PIECE * (half + 1))
            total_ref[:, cols] += dot_of(value, lower_ref[half, rows, :], 1, 0)
        return carry

    lax.fori_loop(0, 8, rise, 0)
    perceptron = total_ref[...] + lower_bias_ref[...]
    dy = dy_ref[...].astype(jnp.float32)
    out_ref[...] = (x1_ref[...] + mod_ref[5:6, :] * perceptron).astype(jnp.bfloat16)
    sums_ref[3:4, :] = token_sum(dy * perceptron)
    dm = (dy * mod_ref[5:6, :]).astype(jnp.bfloat16)
    dm_ref[...] = dm
    sums_ref[5:6, :] = token_sum(dm.astype(jnp.float32))
    total_ref[...] = jnp.zeros_like(total_ref)

    def fall(piece, carry):
        rows = pl.ds(pl.multiple_of(piece * PIECE, PIECE), PIECE)
        grad = jnp.zeros((256, PIECE), jnp.float32)
        for half in range(2):
            cols = slice(PIECE * half, PIECE * (half + 1))
            grad = grad + dot_of(dm_ref[:, cols], lower_ref[half, rows, :], 1, 1)
        grad = (grad * slope_ref[piece]).astype(jnp.bfloat16)
        hidden_sum_ref[piece] = token_sum(grad.astype(jnp.float32))
        total_ref[...] += dot_of(grad, expand_ref[piece], 1, 1)
        expand_grad_ref[piece] = dot_of(a2_ref[...], grad, 0, 0).astype(jnp.bfloat16)
        for half in range(2):
            cols = slice(PIECE * half, PIECE * (half + 1))
            lower_grad_ref[half, rows, :] = dot_of(g_ref[piece], dm_ref[:, cols], 0, 0).astype(
                jnp.bfloat16
            )
        return carry

    lax.fori_loop(0, 8, fall, 0)
    grad = total_ref[...]
    normed, recip = normalize(x1_ref[...])
    sums_ref[1:2, :] = token_sum(grad)
    sums_ref[2:3, :] = token_sum(grad * normed)
    dx1 = dy_ref[...].astype(jnp.float32) + norm_back(
        grad * (1.0 + mod_ref[4:5, :]), normed, recip
    )
    dx1_ref[...] = dx1
    sums_ref[0:1, :] = token_sum(dx1 * att_ref[...])
    datt = (dx1 * mod_ref[2:3, :]).astype(jnp.bfloat16)
    datt_ref[...] = datt
    sums_ref[4:5, :] = token_sum(datt.astype(jnp.float32))


def attention_backward_kernel(
    datt_ref, qkv_ref, lse_ref, o_ref, a1_ref, weight_ref, dqkv_ref, grad_ref, do_ref
):
    do_ref[...] = (
        dot_of(datt_ref[:, :PIECE], weight_ref[6], 1, 1)
        + dot_of(datt_ref[:, PIECE:], weight_ref[7], 1, 1)
    ).astype(jnp.bfloat16)
    masks = head_masks()

    def pair(number, carry):
        at_q = pl.ds(pl.multiple_of(number * 128, 128), 128)
        at_k = pl.ds(pl.multiple_of(number * 128 + 768, 128), 128)
        at_v = pl.ds(pl.multiple_of(number * 128 + 1536, 128), 128)
        queries, key_rows, values = qkv_ref[:, at_q], qkv_ref[:, at_k], qkv_ref[:, at_v]
        blend = do_ref[:, at_q]
        dq = jnp.zeros((256, 128), jnp.float32)
        dk = jnp.zeros((256, 128), jnp.float32)
        dv = jnp.zeros((256, 128), jnp.float32)
        for head in range(2):
            keys_here = key_rows * masks[head]
            scores = dot_of(keys_here, queries, 1, 1) * SCORE_SCALE
            attend = jnp.exp(scores - lse_ref[2 * number + head])
            grad = dot_of(values * masks[head], blend, 1, 1)
            delta = jnp.sum(attend * grad, axis=0, keepdims=True)
            ds = (attend * (grad - delta) * SCORE_SCALE).astype(jnp.bfloat16)
            dv = dv + dot_of(attend.astype(jnp.bfloat16), blend * masks[head], 1, 0)
            dk = dk + dot_of(ds, queries * masks[head], 1, 0)
            dq = dq + dot_of(ds, keys_here, 0, 0)
        dqkv_ref[:, at_q] = dq.astype(jnp.bfloat16)
        dqkv_ref[:, at_k] = dk.astype(jnp.bfloat16)
        dqkv_ref[:, at_v] = dv.astype(jnp.bfloat16)
        return carry

    lax.fori_loop(0, 6, pair, 0)
    for piece in range(6):
        cols = slice(PIECE * piece, PIECE * (piece + 1))
        grad_ref[piece] = dot_of(a1_ref[...], dqkv_ref[:, cols], 0, 0).astype(jnp.bfloat16)
    for half in range(2):
        cols = slice(PIECE * half, PIECE * (half + 1))
        grad_ref[6 + half] = dot_of(o_ref[...], datt_ref[:, cols], 0, 0).astype(jnp.bfloat16)


def input_backward_kernel(dqkv_ref, x_ref, dx1_ref, mod_ref, weight_ref, dx_ref, sums_ref, qkv_sum_ref):
    grad = jnp.zeros((256, 768), jnp.float32)
    for piece in range(6):
        cols = slice(PIECE * piece, PIECE * (piece + 1))
        grad = grad + dot_of(dqkv_ref[:, cols], weight_ref[piece], 1, 1)
    normed, recip = normalize(x_ref[...].astype(jnp.float32))
    sums_ref[0:1, :] = token_sum(grad)
    sums_ref[1:2, :] = token_sum(grad * normed)
    dx_ref[...] = dx1_ref[...] + norm_back(grad * (1.0 + mod_ref[1:2, :]), normed, recip)
    qkv_sum_ref[...] = token_sum(dqkv_ref[...].astype(jnp.float32))


def shaped(shape, dtype=jnp.float32):
    return jax.ShapeDtypeStruct(shape, dtype)


def call_kernel(kernel, outs, args, scratch, flops):
    whole = pl.BlockSpec(memory_space=pltpu.VMEM)
    moved = sum(math.prod(value.shape) * value.dtype.itemsize for value in list(args) + list(outs))
    return pl.pallas_call(
        kernel,
        out_shape=outs,
        in_specs=[whole] * len(args),
        out_specs=tuple(whole for _ in outs),
        scratch_shapes=scratch,
        compiler_params=pltpu.CompilerParams(vmem_limit_bytes=52 * 1024 * 1024),
        cost_estimate=pl.CostEstimate(flops=flops, bytes_accessed=moved, transcendentals=0),
    )(*args)


def attention_forward(x, modulation, weight, biases):
    low, wide = jnp.bfloat16, jnp.float32
    outs = (
        shaped((256, 768), low),
        shaped((256, 2304), low),
        shaped((12, 1, 256)),
        shaped((256, 768), low),
        shaped((256, 768)),
        shaped((256, 768)),
        shaped((256, 768), low),
    )
    return call_kernel(
        attention_forward_kernel, outs, (x, modulation, weight, biases), [], 1500000000
    )


def perceptron(a2, x1, att, dy, modulation, expand, lower, biases, lower_bias):
    low = jnp.bfloat16
    outs = (
        shaped((256, 768), low),
        shaped((256, 768)),
        shaped((256, 768), low),
        shaped((8, 768, PIECE), low),
        shaped((2, 3072, PIECE), low),
        shaped((8, 1, PIECE)),
        shaped((8, 768)),
    )
    scratch = [
        pltpu.VMEM((8, 256, PIECE), low),
        pltpu.VMEM((8, 256, PIECE), jnp.float32),
        pltpu.VMEM((256, 768), low),
        pltpu.VMEM((256, 768), jnp.float32),
    ]
    args = (a2, x1, att, dy, modulation, expand, lower, biases, lower_bias)
    return call_kernel(perceptron_kernel, outs, args, scratch, 7200000000)


def attention_backward(datt, qkv, lse, o, a1, weight):
    low = jnp.bfloat16
    outs = (shaped((256, 2304), low), shaped((8, 768, PIECE), low))
    return call_kernel(
        attention_backward_kernel,
        outs,
        (datt, qkv, lse, o, a1, weight),
        [pltpu.VMEM((256, 768), low)],
        2500000000,
    )


def input_backward(dqkv, x, dx1, modulation, weight):
    outs = (shaped((256, 768)), shaped((8, 768)), shaped((1, 2304)))
    return call_kernel(
        input_backward_kernel, outs, (dqkv, x, dx1, modulation, weight), [], 900000000
    )


def adamw(weight, first_mom, second_mom, gradient, decay):
    new_first = beta_one * first_mom + (1.0 - beta_one) * gradient
    new_second = beta_two * second_mom + (1.0 - beta_two) * gradient * gradient
    update = new_first / correct_one / (jnp.sqrt(new_second / correct_two) + adam_eps)
    return (weight - learn_rate * (update + decay * weight), new_first, new_second)

def index_of(x, y, z, core):
    return (y * 2 + x % 2) * 32 + z * 4 + (x // 2) * 2 + core


def pairs_of(move):
    pairs = []
    for x in range(4):
        for y in range(4):
            for z in range(8):
                for core in range(2):
                    there = move(x, y, z, core)
                    pairs.append((index_of(x, y, z, core), index_of(*there)))
    return pairs


MOVES = {
    "c": pairs_of(lambda x, y, z, core: (x, y, z, 1 - core)),
    "xh": pairs_of(lambda x, y, z, core: (x ^ 2, y, z, core)),
    "xl": pairs_of(lambda x, y, z, core: (x ^ 1, y, z, core)),
    "y0": pairs_of(lambda x, y, z, core: (x, y ^ 1, z, core)),
    "y1": pairs_of(lambda x, y, z, core: (x, 3 - y, z, core)),
    "z0": pairs_of(lambda x, y, z, core: (x, y, z ^ 1, core)),
    "z1": pairs_of(lambda x, y, z, core: (x, y, z ^ 2, core)),
    "z2": pairs_of(lambda x, y, z, core: (x, y, z ^ 4, core)),
    "x+": pairs_of(lambda x, y, z, core: ((x + 1) % 4, y, z, core)),
    "x-": pairs_of(lambda x, y, z, core: ((x + 3) % 4, y, z, core)),
    "y+": pairs_of(lambda x, y, z, core: (x, (y + 1) % 4, z, core)),
    "x2": pairs_of(lambda x, y, z, core: (x ^ 2, y, z, core)),
    "y2": pairs_of(lambda x, y, z, core: (x, y ^ 2, z, core)),
    "y-": pairs_of(lambda x, y, z, core: (x, (y + 3) % 4, z, core)),
}
BLOCK = 24
PIECE = 384


def place(rep, shard):
    y, xl = rep >> 1, rep & 1
    z, xh, c = shard >> 2, (shard >> 1) & 1, shard & 1
    return {
        "z2": z >> 2,
        "z1": (z >> 1) & 1,
        "z0": z & 1,
        "xh": xh,
        "c": c,
        "xl": xl,
        "y0": y & 1,
        "y1": y >> 1,
        "x": xh * 2 + xl,
        "y": y,
    }


def swap(values, move):
    return lax.ppermute(values, ("rep", "shard"), MOVES[move])


def tie(*values):
    return lax.optimization_barrier(values)


def join(mine, theirs, here, axis):
    low = jnp.where(here == 0, mine, theirs)
    high = jnp.where(here == 0, theirs, mine)
    return jnp.concatenate([low, high], axis=axis)


def gather(values, bit, here, axis):
    return join(values, swap(values, bit), here[bit], axis)


def take_half(values, which, axis):
    half = values.shape[axis] // 2
    return lax.dynamic_slice_in_dim(values, which * half, half, axis)


def add_up(*terms):
    total = terms[0].astype(jnp.float32)
    for term in terms[1:]:
        total = total + term.astype(jnp.float32)
    return total.astype(terms[0].dtype)


def scatter(values, bit, here, axis):
    sent = take_half(values, 1 - here[bit], axis)
    kept = take_half(values, here[bit], axis)
    return add_up(kept, swap(sent, bit))


def assemble_kernel(*refs):
    inputs, (first, second, down), sems = refs[:20], refs[20:23], refs[23]
    rep, shard = lax.axis_index("rep"), lax.axis_index("shard")
    y, x = rep // 2, ((shard // 2) % 2) * 2 + rep % 2
    c = shard % 2
    steps = (0, 1, 3, 2, 2)
    for stream in range(2):
        for side in range(2):
            core = c if side == 0 else 1 - c
            for kind in range(5):
                ref = inputs[(stream * 2 + side) * 5 + kind]
                z_start = 4 * stream + (2 if kind == 4 else 0)
                z_count = 2 if kind >= 3 else 4
                for other in range(4):
                    ahead, inner = steps[kind], (0, 1, 2, 3)[other]
                    x_at = (x + (inner if stream == 0 else ahead)) % 4
                    y_at = (y + (ahead if stream == 0 else inner)) % 4
                    xh, xl = x_at // 2, x_at % 2
                    zs = pl.ds(z_start, z_count)
                    for part in range(3):
                        if part == 2:
                            target = down.at[xl, zs, xh, core, y_at]
                        else:
                            target = (first, second)[part].at[y_at, xl, zs, xh, core]
                        pltpu.make_async_copy(ref.at[other, part], target, sems.at[part]).start()
    for part, out in enumerate((first, second, down)):
        pltpu.make_async_copy(out, out, sems.at[part]).wait()


def assemble(pieces):
    shape = jax.ShapeDtypeStruct((4, 2, 8, 2, 2, BLOCK, PIECE), jnp.bfloat16)
    down = jax.ShapeDtypeStruct((2, 8, 2, 2, 4, BLOCK, PIECE), jnp.bfloat16)
    return pl.pallas_call(
        assemble_kernel,
        out_shape=(shape, shape, down),
        in_specs=[pl.BlockSpec(memory_space=pl.ANY)] * 20,
        out_specs=[pl.BlockSpec(memory_space=pltpu.VMEM)] * 3,
        scratch_shapes=[pltpu.SemaphoreType.DMA((3,))],
        compiler_params=pltpu.CompilerParams(vmem_limit_bytes=48 * 1024 * 1024),
        cost_estimate=pl.CostEstimate(flops=0, bytes_accessed=30000000, transcendentals=0),
    )(*pieces)


def own_pieces(rows_weight, down_weight, rep):
    return jnp.stack(
        [
            lax.dynamic_slice(rows_weight, (0, 4608 + PIECE * rep), (BLOCK, PIECE)),
            lax.dynamic_slice(rows_weight, (0, 7680 + PIECE * rep), (BLOCK, PIECE)),
            lax.dynamic_slice(
                down_weight, (BLOCK * (rep >> 1), PIECE * (rep & 1)), (BLOCK, PIECE)
            ),
        ]
    ).astype(jnp.bfloat16)


def ring_round_one(block, axis):
    return swap(block, axis + "+"), swap(block, axis + "-")


def ring_round_two(before, after, axis, cut_axis):
    half = before.shape[cut_axis] // 2
    low = lax.slice_in_dim(before, 0, half, axis=cut_axis)
    high = lax.slice_in_dim(after, half, 2 * half, axis=cut_axis)
    return swap(low, axis + "+"), swap(high, axis + "-")


def gather_weights(values, here):
    blocks = [values[4 * k : 4 * k + 4].transpose(1, 0, 2, 3)[None] for k in range(2)]
    first_axes, last_axes = ("x", "y"), ("y", "x")
    blocks = [
        jnp.concatenate(
            [blocks[k]] + [swap(blocks[k], first_axes[k] + step) for step in ("-", "2", "+")],
            axis=0,
        )
        for k in range(2)
    ]
    near = [ring_round_one(blocks[k], last_axes[k]) for k in range(2)]
    far = [ring_round_two(*near[k], last_axes[k], 2) for k in range(2)]
    pieces = []
    for k in range(2):
        mine = [blocks[k], near[k][1], near[k][0], far[k][0], far[k][1]]
        pieces += mine + [swap(piece, "c") for piece in mine]
    return assemble(pieces)


def core_step(rows_parts, down_parts, here):
    sums = []
    for part in rows_parts:
        part = part.reshape(4, 2, 8, 2, 2, BLOCK, PIECE).transpose(4, 3, 1, 0, 2, 5, 6)
        sums.append(part.reshape(2, 4, 4, 8, BLOCK, PIECE))
    for part in down_parts:
        part = part.reshape(2, 8, 2, 2, 4, BLOCK, PIECE).transpose(3, 2, 0, 4, 1, 5, 6)
        sums.append(part.reshape(2, 4, 4, 8, BLOCK, PIECE))
    stacked = jnp.stack(sums, axis=3)
    sent = lax.dynamic_index_in_dim(stacked, 1 - here["c"], 0, keepdims=False)
    kept = lax.dynamic_index_in_dim(stacked, here["c"], 0, keepdims=False)
    total = add_up(kept, swap(sent, "c"))
    return total[:, :, :, :4], total[:, :, :, 4:].transpose(1, 0, 2, 3, 4, 5)


def at(parts, which):
    found = [lax.dynamic_index_in_dim(part, which % 4, 0, keepdims=False) for part in parts]
    return jnp.concatenate(found, axis=-4) if len(found) > 1 else found[0]


def cut(values):
    half = values.shape[-3] // 2
    return values[..., :half, :, :], values[..., half:, :, :]


def scatter_one(parts, axis, here):
    low, high = cut(at(parts, here[axis] + 2))
    return swap(low, axis + "+"), swap(high, axis + "-")


def scatter_two(parts, passed, axis, here):
    low, high = passed
    ahead_low, ahead_high = cut(at(parts, here[axis] + 1))
    ahead = jnp.concatenate([add_up(ahead_low, low), ahead_high], axis=-3)
    back_low, back_high = cut(at(parts, here[axis] + 3))
    back = jnp.concatenate([back_low, add_up(back_high, high)], axis=-3)
    return add_up(at(parts, here[axis]), swap(ahead, axis + "+"), swap(back, axis + "-"))


def scatter_direct(values, axis, here):
    parts = [values]
    return add_up(
        at(parts, here[axis]),
        swap(at(parts, here[axis] + 1), axis + "+"),
        swap(at(parts, here[axis] + 3), axis + "-"),
        swap(at(parts, here[axis] + 2), axis + "2"),
    )


def scatter_places(streams, here):
    axes = (("x", "y"), ("y", "x"))
    passed = [scatter_one(streams[k], axes[k][0], here) for k in range(2)]
    streams = [scatter_two(streams[k], passed[k], axes[k][0], here) for k in range(2)]
    streams = [scatter_direct(streams[k], axes[k][1], here) for k in range(2)]
    return jnp.concatenate(streams, axis=1)


def scatter_z(values, here):
    number = values.shape[0]
    values = values.reshape(number, 2, 2, 2, BLOCK, PIECE)
    for bit, axis in (("z0", 3), ("z1", 2), ("z2", 1)):
        values = scatter(values, bit, here, axis)
    return values.reshape(number, BLOCK, PIECE)


def gather_pieces(values, here):
    number = values.shape[0]
    values = values.reshape(1, 1, number, BLOCK, PIECE)
    values = gather(values, "xl", here, 1)
    before, after = swap(values, "y+"), swap(values, "y-")
    far = swap(before, "y+")
    ring = jnp.concatenate([values, after, far, before, values, after, far], axis=0)
    ring = lax.dynamic_slice_in_dim(ring, (4 - here["y"]) % 4, 4, axis=0)
    return ring.reshape(8, number, BLOCK, PIECE)


def condition(step_ids, class_ids, class_table):
    half_width = class_table.shape[1] // 2
    frequency = jnp.exp(
        -math.log(10000.0) * jnp.arange(half_width).astype(jnp.float32) / half_width
    )
    angles = step_ids.astype(jnp.float32)[:, None] * frequency[None, :]
    time_embed = jnp.concatenate([jnp.cos(angles), jnp.sin(angles)], axis=1)
    label_rows = jnp.take(class_table, class_ids, axis=0).astype(jnp.float32)
    return jax.nn.silu(time_embed + label_rows).astype(jnp.bfloat16)


def condition_kernel(act_ref, weight_ref, out_ref):
    out_ref[...] = jnp.dot(act_ref[...], weight_ref[...], preferred_element_type=jnp.float32)


def modulate(cond_act, weight):
    rows = jnp.broadcast_to(cond_act, (16, cond_act.shape[1]))
    out = pl.pallas_call(
        condition_kernel,
        grid=(5,),
        in_specs=[
            pl.BlockSpec(rows.shape, lambda k: (0, 0)),
            pl.BlockSpec((weight.shape[0], 1024), lambda k: (0, k)),
        ],
        out_specs=pl.BlockSpec((16, 1024), lambda k: (0, k)),
        out_shape=jax.ShapeDtypeStruct((16, weight.shape[1]), jnp.float32),
    )(rows, weight)
    return out[0]


def local(
    latents,
    cotangent,
    step_ids,
    class_ids,
    class_table,
    rows_weight,
    down_weight,
    bias_weight,
    rows_first,
    down_first,
    bias_first,
    rows_second,
    down_second,
    bias_second,
):
    rep, shard = lax.axis_index("rep"), lax.axis_index("shard")
    here = place(rep, shard)
    width = latents.shape[-1]
    bias_here = jnp.pad(bias_weight.reshape(BLOCK, 15), ((0, 0), (0, 497)))
    ada_here = jnp.concatenate([rows_weight[:, : 6 * width], bias_here], axis=1)
    ada_whole = lax.all_gather(ada_here.astype(jnp.bfloat16), "shard", axis=0, tiled=True)
    biases = ada_whole[:, 6 * width : 6 * width + 15].astype(jnp.float32).reshape(-1)
    cond_act = condition(step_ids, class_ids, class_table)
    modulation = modulate(cond_act, ada_whole)[: 6 * width]
    modulation = modulation + biases[: 6 * width]
    blocks = own_pieces(rows_weight, down_weight, rep).reshape(1, 1, 1, 3, BLOCK, PIECE)
    for axis, bit in ((0, "z2"), (1, "z1"), (2, "z0")):
        blocks = gather(blocks, bit, here, axis)
    first, second, lower = gather_weights(blocks.reshape(8, 3, BLOCK, PIECE), here)
    first, second = first.reshape(8, 768, PIECE), second.reshape(8, 768, PIECE)
    lower = lower.reshape(2, 3072, PIECE)
    modulation = jnp.pad(modulation.reshape(6, width), ((0, 2), (0, 0)))
    x, dy = latents[0], cotangent[0]
    a1, qkv, lse, o, att, x1, a2 = attention_forward(
        x, modulation, first, biases[6 * width : 10 * width].reshape(8, 1, PIECE)
    )
    output, dx1, datt, expand_grad, lower_grad, hidden_sum, sums = perceptron(
        a2,
        x1,
        att,
        dy,
        modulation,
        second,
        lower,
        biases[10 * width : 14 * width].reshape(8, 1, PIECE),
        biases[14 * width :].reshape(1, width),
    )
    early = core_step([expand_grad], [lower_grad], here)
    dqkv, first_grad = attention_backward(datt, qkv, lse, o, a1, first)
    early, dqkv, first_grad = tie(early, dqkv, first_grad)
    late = core_step([first_grad], [], here)
    dx, late_sums, qkv_sum = input_backward(dqkv, x, dx1, modulation, first)
    streams = [list(parts) for parts in zip(late, early)]
    output, grad_latents = output[None], dx[None]
    dmod = jnp.concatenate([late_sums[:2], sums[:4]], axis=0).reshape(-1)
    dmod = dmod.astype(jnp.bfloat16).astype(jnp.float32)
    bias_term = jnp.concatenate(
        [dmod, qkv_sum.reshape(-1), sums[4], hidden_sum.reshape(-1), sums[5]]
    )
    vector = jnp.concatenate(
        [bias_term, cond_act.reshape(-1).astype(jnp.float32), jnp.zeros((4096,), jnp.float32)]
    )
    vectors = lax.all_gather(vector[None], "shard", axis=0, tiled=True)
    cond_columns = lax.dynamic_slice(vectors, (0, 15 * width + BLOCK * shard), (32, BLOCK))
    owned = scatter_z(scatter_places(streams, here), here)
    owned = gather_pieces(owned, here).astype(jnp.float32)
    ada_term = lax.dot_general(
        cond_columns.astype(jnp.bfloat16),
        vectors[:, : 6 * width].astype(jnp.bfloat16),
        (((0,), (0,)), ((), ())),
        preferred_element_type=jnp.float32,
    )
    bias_sum = jnp.sum(vectors[:, : 15 * width], axis=0)
    bias_sum = lax.dynamic_slice(bias_sum, (360 * shard,), (360,))
    packed = jnp.concatenate(
        [ada_term, jnp.pad(bias_sum, (0, 24)).reshape(3, 128).repeat(8, axis=0)], axis=1
    ).astype(jnp.bfloat16)
    for bit in ("xl", "y0", "y1"):
        packed = add_up(packed, swap(packed, bit))
    packed = packed.astype(jnp.float32)
    factor = 1.0 / 65536
    grad_rows = (
        jnp.concatenate(
            [packed[:, : 6 * width]]
            + [owned[piece, 0] for piece in range(8)]
            + [owned[piece, 1] for piece in range(8)],
            axis=1,
        )
        * factor
    )
    grad_down = (
        jnp.concatenate(
            [
                jnp.concatenate([owned[2 * row, 2], owned[2 * row + 1, 2]], axis=1)
                for row in range(4)
            ],
            axis=0,
        )
        * factor
    )
    grad_bias = packed[::8, 6 * width :].reshape(-1)[:360] * factor
    new_rows, first_rows, second_rows = adamw(
        rows_weight, rows_first, rows_second, grad_rows, decay_rate
    )
    new_down, first_down, second_down = adamw(
        down_weight, down_first, down_second, grad_down, decay_rate
    )
    new_bias, first_bias, second_bias = adamw(bias_weight, bias_first, bias_second, grad_bias, 0.0)
    return (
        output,
        grad_latents,
        grad_rows,
        grad_down,
        grad_bias,
        new_rows,
        new_down,
        new_bias,
        first_rows,
        first_down,
        first_bias,
        second_rows,
        second_down,
        second_bias,
    )


def solution(mesh):
    placed = (
        P(("rep", "shard"), None, None),
        P(("rep", "shard"), None, None),
        P(("rep", "shard")),
        P(("rep", "shard")),
        P(),
        P("shard", None),
        P("shard", None),
        P("shard"),
        P("shard", None),
        P("shard", None),
        P("shard"),
        P("shard", None),
        P("shard", None),
        P("shard"),
    )
    return jax.shard_map(
        local,
        mesh=mesh,
        in_specs=placed,
        out_specs=(
            P(("rep", "shard"), None, None),
            P(("rep", "shard"), None, None),
            P("shard", None),
            P("shard", None),
            P("shard"),
            P("shard", None),
            P("shard", None),
            P("shard"),
            P("shard", None),
            P("shard", None),
            P("shard"),
            P("shard", None),
            P("shard", None),
            P("shard"),
        ),
        check_vma=False,
    )
```

```python
import math

import jax
import jax.numpy as jnp
from jax import lax
from jax.experimental import pallas as pl
from jax.experimental.pallas import tpu as pltpu
from jax.sharding import PartitionSpec as P

HEAD_FEATURES = 64


norm_eps = 1e-06
gelu_coef = math.sqrt(2.0 / math.pi)
learn_rate = 0.05
beta_one = 0.9
beta_two = 0.95
adam_eps = 1e-08
decay_rate = 0.1
correct_one = 1.0 - 0.9**3
correct_two = 1.0 - 0.95**3


def matmul_result(pattern, first_op, second_op):
    return jnp.einsum(pattern, first_op, second_op, preferred_element_type=jnp.float32)


def normalize(values):
    centred = values - jnp.mean(values, axis=-1, keepdims=True)
    recip = lax.rsqrt(jnp.mean(centred * centred, axis=-1, keepdims=True) + norm_eps)
    return (centred * recip, recip)


def norm_back(grad_normed, normed, recip):
    return recip * (
        grad_normed
        - jnp.mean(grad_normed, axis=-1, keepdims=True)
        - normed * jnp.mean(grad_normed * normed, axis=-1, keepdims=True)
    )


def gelu_pair(preactivation):
    tanh_value = jnp.tanh(
        gelu_coef * (preactivation + 0.044715 * preactivation * preactivation * preactivation)
    )
    result = 0.5 * preactivation * (1.0 + tanh_value)
    slopes = 0.5 * (1.0 + tanh_value) + 0.5 * preactivation * (
        1.0 - tanh_value * tanh_value
    ) * gelu_coef * (1.0 + 3.0 * 0.044715 * preactivation * preactivation)
    return (result, slopes)


def dot_of(left, right, left_axis, right_axis):
    return lax.dot_general(
        left,
        right,
        (((left_axis,), (right_axis,)), ((), ())),
        preferred_element_type=jnp.float32,
    )


def token_sum(values):
    return jnp.sum(values, axis=0, keepdims=True)


ADA_BIAS, QKV_BIAS, ATT_BIAS, HIDDEN_BIAS, DOWN_BIAS = 0, 4608, 6912, 7680, 10752


def mod_row(mod_ref, bias_ref, number):
    cols = slice(768 * number, 768 * (number + 1))
    return mod_ref[:, cols] + bias_ref[:, cols]


def head_masks():
    lane = lax.broadcasted_iota(jnp.int32, (1, 2 * HEAD_FEATURES), 1)
    return [(lane // HEAD_FEATURES == head).astype(jnp.bfloat16) for head in range(2)]


SCORE_SCALE = 1.0 / math.sqrt(HEAD_FEATURES)


def attention_forward_kernel(
    x_ref, mod_ref, bias_ref, weight_ref, a1_ref, qkv_ref, lse_ref, o_ref, att_ref, x1_ref, a2_ref
):
    x = x_ref[...].astype(jnp.float32)
    normed, _ = normalize(x)
    shift, scale = mod_row(mod_ref, bias_ref, 0), mod_row(mod_ref, bias_ref, 1)
    a1_ref[...] = (normed * (1.0 + scale) + shift).astype(jnp.bfloat16)
    for piece in range(6):
        cols = slice(PIECE * piece, PIECE * (piece + 1))
        bias = bias_ref[:, QKV_BIAS + PIECE * piece : QKV_BIAS + PIECE * (piece + 1)]
        product = dot_of(a1_ref[...], weight_ref[piece], 1, 0) + bias
        qkv_ref[:, cols] = product.astype(jnp.bfloat16)
    masks = head_masks()

    def pair(number, carry):
        at_q = pl.ds(pl.multiple_of(number * 128, 128), 128)
        at_k = pl.ds(pl.multiple_of(number * 128 + 768, 128), 128)
        at_v = pl.ds(pl.multiple_of(number * 128 + 1536, 128), 128)
        queries, key_rows, values = qkv_ref[:, at_q], qkv_ref[:, at_k], qkv_ref[:, at_v]
        total = jnp.zeros((256, 128), jnp.float32)
        for head in range(2):
            scores = dot_of(key_rows * masks[head], queries, 1, 1) * SCORE_SCALE
            top = jnp.max(scores, axis=0, keepdims=True)
            lse = top + jnp.log(jnp.sum(jnp.exp(scores - top), axis=0, keepdims=True))
            lse_ref[2 * number + head] = lse
            attend = jnp.exp(scores - lse).astype(jnp.bfloat16)
            total = total + dot_of(attend, values * masks[head], 0, 0)
        o_ref[:, at_q] = total.astype(jnp.bfloat16)
        return carry

    lax.fori_loop(0, 6, pair, 0)
    gate = mod_row(mod_ref, bias_ref, 2)
    for half in range(2):
        cols = slice(PIECE * half, PIECE * (half + 1))
        bias = bias_ref[:, ATT_BIAS + PIECE * half : ATT_BIAS + PIECE * (half + 1)]
        att = dot_of(o_ref[...], weight_ref[6 + half], 1, 0) + bias
        att_ref[:, cols] = att
        x1_ref[:, cols] = x_ref[:, cols].astype(jnp.float32) + gate[:, cols] * att
    normed, _ = normalize(x1_ref[...])
    shift, scale = mod_row(mod_ref, bias_ref, 3), mod_row(mod_ref, bias_ref, 4)
    a2_ref[...] = (normed * (1.0 + scale) + shift).astype(jnp.bfloat16)


def perceptron_kernel(
    a2_ref,
    x1_ref,
    att_ref,
    dy_ref,
    mod_ref,
    expand_ref,
    lower_ref,
    bias_ref,
    out_ref,
    dx1_ref,
    datt_ref,
    expand_grad_ref,
    lower_grad_ref,
    hidden_sum_ref,
    sums_ref,
    g_ref,
    slope_ref,
    dm_ref,
    total_ref,
    turned_ref,
):
    total_ref[...] = jnp.zeros_like(total_ref)
    turned_ref[...] = a2_ref[...].T

    def rise(piece, carry):
        at_bias = pl.ds(pl.multiple_of(HIDDEN_BIAS + piece * PIECE, 128), PIECE)
        hidden = dot_of(a2_ref[...], expand_ref[piece], 1, 0) + bias_ref[:, at_bias]
        value, slope = gelu_pair(hidden)
        value = value.astype(jnp.bfloat16)
        g_ref[piece] = value
        slope_ref[piece] = slope
        rows = pl.ds(pl.multiple_of(piece * PIECE, PIECE), PIECE)
        for half in range(2):
            cols = slice(PIECE * half, PIECE * (half + 1))
            total_ref[:, cols] += dot_of(value, lower_ref[half, rows, :], 1, 0)
        return carry

    lax.fori_loop(0, 8, rise, 0)
    perceptron = total_ref[...] + bias_ref[:, DOWN_BIAS:]
    gate = mod_row(mod_ref, bias_ref, 5)
    dy = dy_ref[...].astype(jnp.float32)
    out_ref[...] = (x1_ref[...] + gate * perceptron).astype(jnp.bfloat16)
    sums_ref[3:4, :] = token_sum(dy * perceptron)
    dm = (dy * gate).astype(jnp.bfloat16)
    dm_ref[...] = dm
    sums_ref[5:6, :] = token_sum(dm.astype(jnp.float32))
    total_ref[...] = jnp.zeros_like(total_ref)

    def fall(piece, carry):
        rows = pl.ds(pl.multiple_of(piece * PIECE, PIECE), PIECE)
        grad = jnp.zeros((256, PIECE), jnp.float32)
        for half in range(2):
            cols = slice(PIECE * half, PIECE * (half + 1))
            grad = grad + dot_of(dm_ref[:, cols], lower_ref[half, rows, :], 1, 1)
        grad = (grad * slope_ref[piece]).astype(jnp.bfloat16)
        hidden_sum_ref[piece] = token_sum(grad.astype(jnp.float32))
        total_ref[...] += dot_of(grad, expand_ref[piece], 1, 1)
        expand_grad_ref[piece] = dot_of(turned_ref[...], grad, 1, 0).astype(jnp.bfloat16)
        for half in range(2):
            cols = slice(PIECE * half, PIECE * (half + 1))
            lower_grad_ref[half, rows, :] = dot_of(g_ref[piece], dm_ref[:, cols], 0, 0).astype(
                jnp.bfloat16
            )
        return carry

    lax.fori_loop(0, 8, fall, 0)
    grad = total_ref[...]
    normed, recip = normalize(x1_ref[...])
    sums_ref[1:2, :] = token_sum(grad)
    sums_ref[2:3, :] = token_sum(grad * normed)
    dx1 = dy_ref[...].astype(jnp.float32) + norm_back(
        grad * (1.0 + mod_row(mod_ref, bias_ref, 4)), normed, recip
    )
    dx1_ref[...] = dx1
    sums_ref[0:1, :] = token_sum(dx1 * att_ref[...])
    datt = (dx1 * mod_row(mod_ref, bias_ref, 2)).astype(jnp.bfloat16)
    datt_ref[...] = datt
    sums_ref[4:5, :] = token_sum(datt.astype(jnp.float32))


def attention_backward_kernel(
    datt_ref, qkv_ref, lse_ref, o_ref, a1_ref, weight_ref, dqkv_ref, grad_ref, do_ref
):
    do_ref[...] = (
        dot_of(datt_ref[:, :PIECE], weight_ref[6], 1, 1)
        + dot_of(datt_ref[:, PIECE:], weight_ref[7], 1, 1)
    ).astype(jnp.bfloat16)
    masks = head_masks()

    def pair(number, carry):
        at_q = pl.ds(pl.multiple_of(number * 128, 128), 128)
        at_k = pl.ds(pl.multiple_of(number * 128 + 768, 128), 128)
        at_v = pl.ds(pl.multiple_of(number * 128 + 1536, 128), 128)
        queries, key_rows, values = qkv_ref[:, at_q], qkv_ref[:, at_k], qkv_ref[:, at_v]
        blend = do_ref[:, at_q]
        dq = jnp.zeros((256, 128), jnp.float32)
        dk = jnp.zeros((256, 128), jnp.float32)
        dv = jnp.zeros((256, 128), jnp.float32)
        for head in range(2):
            keys_here = key_rows * masks[head]
            scores = dot_of(keys_here, queries, 1, 1) * SCORE_SCALE
            attend = jnp.exp(scores - lse_ref[2 * number + head])
            grad = dot_of(values * masks[head], blend, 1, 1)
            delta = jnp.sum(attend * grad, axis=0, keepdims=True)
            ds = (attend * (grad - delta) * SCORE_SCALE).astype(jnp.bfloat16)
            dv = dv + dot_of(attend.astype(jnp.bfloat16), blend * masks[head], 1, 0)
            dk = dk + dot_of(ds, queries * masks[head], 1, 0)
            dq = dq + dot_of(ds, keys_here, 0, 0)
        dqkv_ref[:, at_q] = dq.astype(jnp.bfloat16)
        dqkv_ref[:, at_k] = dk.astype(jnp.bfloat16)
        dqkv_ref[:, at_v] = dv.astype(jnp.bfloat16)
        return carry

    lax.fori_loop(0, 6, pair, 0)
    for piece in range(6):
        cols = slice(PIECE * piece, PIECE * (piece + 1))
        grad_ref[piece] = dot_of(a1_ref[...], dqkv_ref[:, cols], 0, 0).astype(jnp.bfloat16)
    for half in range(2):
        cols = slice(PIECE * half, PIECE * (half + 1))
        grad_ref[6 + half] = dot_of(o_ref[...], datt_ref[:, cols], 0, 0).astype(jnp.bfloat16)


def input_backward_kernel(
    dqkv_ref, x_ref, dx1_ref, mod_ref, bias_ref, weight_ref, sums_ref, hidden_sum_ref, dx_ref, vector_ref
):
    grad = jnp.zeros((256, 768), jnp.float32)
    for piece in range(6):
        cols = slice(PIECE * piece, PIECE * (piece + 1))
        grad = grad + dot_of(dqkv_ref[:, cols], weight_ref[piece], 1, 1)
    normed, recip = normalize(x_ref[...].astype(jnp.float32))
    scale = mod_row(mod_ref, bias_ref, 1)
    dx_ref[...] = dx1_ref[...] + norm_back(grad * (1.0 + scale), normed, recip)

    def rounded(row):
        return row.astype(jnp.bfloat16).astype(jnp.float32)

    vector_ref[:, :768] = rounded(token_sum(grad))
    vector_ref[:, 768:1536] = rounded(token_sum(grad * normed))
    for row in range(4):
        vector_ref[:, 1536 + 768 * row : 2304 + 768 * row] = rounded(sums_ref[row : row + 1, :])
    vector_ref[:, QKV_BIAS:ATT_BIAS] = token_sum(dqkv_ref[...].astype(jnp.float32))
    vector_ref[:, ATT_BIAS:HIDDEN_BIAS] = sums_ref[4:5, :]
    for piece in range(8):
        cols = slice(HIDDEN_BIAS + PIECE * piece, HIDDEN_BIAS + PIECE * (piece + 1))
        vector_ref[:, cols] = hidden_sum_ref[piece]
    vector_ref[:, DOWN_BIAS : DOWN_BIAS + 768] = sums_ref[5:6, :]


VECTOR = 11520


def adamw_rows(refs, cols, rows, grad):
    weight, first, second, out_grad, new, new_first, new_second = refs
    results = adamw(weight[rows, cols], first[rows, cols], second[rows, cols], grad, decay_rate)
    out_grad[rows, cols] = grad
    new[rows, cols], new_first[rows, cols], new_second[rows, cols] = results


def update_kernel(
    ada_ref,
    owned_ref,
    rows_weight,
    rows_first,
    rows_second,
    down_weight,
    down_first,
    down_second,
    grad_rows,
    new_rows,
    first_rows,
    second_rows,
    grad_down,
    new_down,
    first_down,
    second_down,
):
    factor = 1.0 / 65536
    y = lax.axis_index("rep") // 2
    rows_refs = (
        rows_weight, rows_first, rows_second, grad_rows, new_rows, first_rows, second_rows
    )
    down_refs = (
        down_weight, down_first, down_second, grad_down, new_down, first_down, second_down
    )
    every = slice(0, BLOCK)
    for piece in range(12):
        cols = slice(PIECE * piece, PIECE * (piece + 1))
        adamw_rows(rows_refs, cols, every, ada_ref[:, cols] * factor)
    for piece in range(8):
        place = lax.rem(piece // 2 - y + 4, 4)
        found = [owned_ref[place, piece % 2, part] * factor for part in range(3)]
        cols = slice(4608 + PIECE * piece, 4608 + PIECE * (piece + 1))
        adamw_rows(rows_refs, cols, every, found[0])
        cols = slice(7680 + PIECE * piece, 7680 + PIECE * (piece + 1))
        adamw_rows(rows_refs, cols, every, found[1])
        cols = slice(PIECE * (piece % 2), PIECE * (piece % 2 + 1))
        rows = slice(BLOCK * (piece // 2), BLOCK * (piece // 2 + 1))
        adamw_rows(down_refs, cols, rows, found[2])


def shaped(shape, dtype=jnp.float32):
    return jax.ShapeDtypeStruct(shape, dtype)


def call_kernel(kernel, outs, args, scratch, flops):
    whole = pl.BlockSpec(memory_space=pltpu.VMEM)
    moved = sum(math.prod(value.shape) * value.dtype.itemsize for value in list(args) + list(outs))
    return pl.pallas_call(
        kernel,
        out_shape=outs,
        in_specs=[whole] * len(args),
        out_specs=tuple(whole for _ in outs),
        scratch_shapes=scratch,
        compiler_params=pltpu.CompilerParams(vmem_limit_bytes=52 * 1024 * 1024),
        cost_estimate=pl.CostEstimate(flops=flops, bytes_accessed=moved, transcendentals=0),
    )(*args)


def attention_forward(x, modulation, biases, weight):
    low, wide = jnp.bfloat16, jnp.float32
    outs = (
        shaped((256, 768), low),
        shaped((256, 2304), low),
        shaped((12, 1, 256)),
        shaped((256, 768), low),
        shaped((256, 768)),
        shaped((256, 768)),
        shaped((256, 768), low),
    )
    return call_kernel(
        attention_forward_kernel, outs, (x, modulation, biases, weight), [], 1500000000
    )


def perceptron(a2, x1, att, dy, modulation, expand, lower, biases):
    low = jnp.bfloat16
    outs = (
        shaped((256, 768), low),
        shaped((256, 768)),
        shaped((256, 768), low),
        shaped((8, 768, PIECE), low),
        shaped((2, 3072, PIECE), low),
        shaped((8, 1, PIECE)),
        shaped((8, 768)),
    )
    scratch = [
        pltpu.VMEM((8, 256, PIECE), low),
        pltpu.VMEM((8, 256, PIECE), jnp.float32),
        pltpu.VMEM((256, 768), low),
        pltpu.VMEM((256, 768), jnp.float32),
        pltpu.VMEM((768, 256), low),
    ]
    args = (a2, x1, att, dy, modulation, expand, lower, biases)
    return call_kernel(perceptron_kernel, outs, args, scratch, 7200000000)


def attention_backward(datt, qkv, lse, o, a1, weight):
    low = jnp.bfloat16
    outs = (shaped((256, 2304), low), shaped((8, 768, PIECE), low))
    return call_kernel(
        attention_backward_kernel,
        outs,
        (datt, qkv, lse, o, a1, weight),
        [pltpu.VMEM((256, 768), low)],
        2500000000,
    )


def input_backward(*args):
    outs = (shaped((256, 768)), shaped((1, VECTOR)))
    return call_kernel(input_backward_kernel, outs, args, [], 900000000)


def update(*args):
    outs = tuple(shaped(shape) for shape in 4 * [(BLOCK, 10752)] + 4 * [(96, 768)])
    return call_kernel(update_kernel, outs, args, [], 10000000)


def adamw(weight, first_mom, second_mom, gradient, decay):
    new_first = beta_one * first_mom + (1.0 - beta_one) * gradient
    new_second = beta_two * second_mom + (1.0 - beta_two) * gradient * gradient
    update = new_first / correct_one / (jnp.sqrt(new_second / correct_two) + adam_eps)
    return (weight - learn_rate * (update + decay * weight), new_first, new_second)

def index_of(x, y, z, core):
    return (y * 2 + x % 2) * 32 + z * 4 + (x // 2) * 2 + core


def pairs_of(move):
    pairs = []
    for x in range(4):
        for y in range(4):
            for z in range(8):
                for core in range(2):
                    there = move(x, y, z, core)
                    pairs.append((index_of(x, y, z, core), index_of(*there)))
    return pairs


MOVES = {
    "c": pairs_of(lambda x, y, z, core: (x, y, z, 1 - core)),
    "xh": pairs_of(lambda x, y, z, core: (3 - x, y, z, core)),
    "xl": pairs_of(lambda x, y, z, core: (x ^ 1, y, z, core)),
    "y0": pairs_of(lambda x, y, z, core: (x, y ^ 1, z, core)),
    "y1": pairs_of(lambda x, y, z, core: (x, 3 - y, z, core)),
    "z0": pairs_of(lambda x, y, z, core: (x, y, z ^ 1, core)),
    "z1": pairs_of(lambda x, y, z, core: (x, y, z ^ 2, core)),
    "z2": pairs_of(lambda x, y, z, core: (x, y, z ^ 4, core)),
    "x+": pairs_of(lambda x, y, z, core: ((x + 1) % 4, y, z, core)),
    "x-": pairs_of(lambda x, y, z, core: ((x + 3) % 4, y, z, core)),
    "y+": pairs_of(lambda x, y, z, core: (x, (y + 1) % 4, z, core)),
    "x2": pairs_of(lambda x, y, z, core: (x ^ 2, y, z, core)),
    "y2": pairs_of(lambda x, y, z, core: (x, y ^ 2, z, core)),
    "y-": pairs_of(lambda x, y, z, core: (x, (y + 3) % 4, z, core)),
}
BLOCK = 24
PIECE = 384


def place(rep, shard):
    y, xl = rep >> 1, rep & 1
    z, xh, c = shard >> 2, (shard >> 1) & 1, shard & 1
    return {
        "z2": z >> 2,
        "z1": (z >> 1) & 1,
        "z0": z & 1,
        "xh": xh,
        "c": c,
        "xl": xl,
        "y0": y & 1,
        "y1": y >> 1,
        "x": xh * 2 + xl,
        "y": y,
    }


def swap(values, move):
    return lax.ppermute(values, ("rep", "shard"), MOVES[move])


def tie(*values):
    return lax.optimization_barrier(values)


def join(mine, theirs, here, axis):
    low = jnp.where(here == 0, mine, theirs)
    high = jnp.where(here == 0, theirs, mine)
    return jnp.concatenate([low, high], axis=axis)


def gather(values, bit, here, axis):
    return join(values, swap(values, bit), here[bit], axis)


def take_half(values, which, axis):
    half = values.shape[axis] // 2
    return lax.dynamic_slice_in_dim(values, which * half, half, axis)


def add_up(*terms):
    total = terms[0].astype(jnp.float32)
    for term in terms[1:]:
        total = total + term.astype(jnp.float32)
    return total.astype(terms[0].dtype)


def scatter(values, bit, here, axis):
    sent = take_half(values, 1 - here[bit], axis)
    kept = take_half(values, here[bit], axis)
    return add_up(kept, swap(sent, bit))


def assemble_kernel(*refs):
    inputs, (first, second, down), sems = refs[:20], refs[20:23], refs[23]
    rep, shard = lax.axis_index("rep"), lax.axis_index("shard")
    y, x = rep // 2, ((shard // 2) % 2) * 2 + rep % 2
    c = shard % 2
    steps = (0, 1, 3, 2, 2)
    for stream in range(2):
        for side in range(2):
            core = c if side == 0 else 1 - c
            for kind in range(5):
                ref = inputs[(stream * 2 + side) * 5 + kind]
                z_start = 4 * stream + (2 if kind == 4 else 0)
                z_count = 2 if kind >= 3 else 4
                for other in range(4):
                    ahead, inner = steps[kind], (0, 1, 2, 3)[other]
                    x_at = (x + (inner if stream == 0 else ahead)) % 4
                    y_at = (y + (ahead if stream == 0 else inner)) % 4
                    xh, xl = x_at // 2, x_at % 2
                    zs = pl.ds(z_start, z_count)
                    for part in range(3):
                        if part == 2:
                            target = down.at[xl, zs, xh, core, y_at]
                        else:
                            target = (first, second)[part].at[y_at, xl, zs, xh, core]
                        pltpu.make_async_copy(ref.at[other, part], target, sems.at[part]).start()
    for part, out in enumerate((first, second, down)):
        pltpu.make_async_copy(out, out, sems.at[part]).wait()


def assemble(pieces):
    shape = jax.ShapeDtypeStruct((4, 2, 8, 2, 2, BLOCK, PIECE), jnp.bfloat16)
    down = jax.ShapeDtypeStruct((2, 8, 2, 2, 4, BLOCK, PIECE), jnp.bfloat16)
    return pl.pallas_call(
        assemble_kernel,
        out_shape=(shape, shape, down),
        in_specs=[pl.BlockSpec(memory_space=pl.ANY)] * 20,
        out_specs=[pl.BlockSpec(memory_space=pltpu.VMEM)] * 3,
        scratch_shapes=[pltpu.SemaphoreType.DMA((3,))],
        compiler_params=pltpu.CompilerParams(vmem_limit_bytes=48 * 1024 * 1024),
        cost_estimate=pl.CostEstimate(flops=0, bytes_accessed=30000000, transcendentals=0),
    )(*pieces)


def own_pieces(rows_weight, down_weight, rep):
    return jnp.stack(
        [
            lax.dynamic_slice(rows_weight, (0, 4608 + PIECE * rep), (BLOCK, PIECE)),
            lax.dynamic_slice(rows_weight, (0, 7680 + PIECE * rep), (BLOCK, PIECE)),
            lax.dynamic_slice(
                down_weight, (BLOCK * (rep >> 1), PIECE * (rep & 1)), (BLOCK, PIECE)
            ),
        ]
    ).astype(jnp.bfloat16)


def ring_round_one(block, axis):
    return swap(block, axis + "+"), swap(block, axis + "-")


def ring_round_two(before, after, axis, cut_axis):
    half = before.shape[cut_axis] // 2
    low = lax.slice_in_dim(before, 0, half, axis=cut_axis)
    high = lax.slice_in_dim(after, half, 2 * half, axis=cut_axis)
    return swap(low, axis + "+"), swap(high, axis + "-")


def gather_weights(values, small, partial_of, here):
    blocks = [values[4 * k : 4 * k + 4].transpose(1, 0, 2, 3)[None] for k in range(2)]
    first_axes, last_axes = ("x", "y"), ("y", "x")
    direct = [[swap(blocks[k], first_axes[k] + step) for step in ("-", "2", "+")] for k in range(2)]
    direct, small = tie(direct, small)
    blocks = [
        jnp.concatenate([blocks[k]] + direct[k], axis=0) for k in range(2)
    ]
    near = [ring_round_one(blocks[k], last_axes[k]) for k in range(2)]
    (partial, columns), biases = partial_of(small)
    for bit, axis in (("c", 4), ("xh", 3), ("z0", 2)):
        partial = scatter(partial, bit, here, axis)
    near, partial, biases = tie(near, partial, biases)
    far = [ring_round_two(*near[k], last_axes[k], 2) for k in range(2)]
    for bit, axis in (("z1", 1), ("z2", 0)):
        partial = scatter(partial, bit, here, axis)
    pieces = []
    for k in range(2):
        mine = [blocks[k], near[k][1], near[k][0], far[k][0], far[k][1]]
        pieces += mine + [swap(piece, "c") for piece in mine]
    return assemble(pieces), partial.reshape(1, -1), biases, columns


ROWS_SHAPE = (4, 2, 8, 2, 2, BLOCK, PIECE)
DOWN_SHAPE = (2, 8, 2, 2, 4, BLOCK, PIECE)


def core_swap(gradient, shape, here):
    gradient = gradient.reshape(shape)
    axis = 4 if shape is ROWS_SHAPE else 3
    sent = lax.dynamic_index_in_dim(gradient, 1 - here["c"], axis, keepdims=True)
    return gradient, swap(sent, "c"), shape


def place_block(part, axis, which, zs, here):
    whole, received, shape = part
    first, count = zs
    xh, xl = which // 2, which % 2
    found = []
    for values, core in ((whole, here["c"]), (received, 0)):
        if axis == "x":
            if shape is ROWS_SHAPE:
                start, size = (0, xl, first, xh, core, 0, 0), (4, 1, count, 1, 1, BLOCK, PIECE)
            else:
                start, size = (xl, first, xh, core, 0, 0, 0), (1, count, 1, 1, 4, BLOCK, PIECE)
        elif shape is ROWS_SHAPE:
            start, size = (which, 0, first, 0, core, 0, 0), (1, 2, count, 2, 1, BLOCK, PIECE)
        else:
            start, size = (0, first, 0, core, which, 0, 0), (2, count, 2, 1, 1, BLOCK, PIECE)
        block = lax.dynamic_slice(values, start, size)
        if axis == "x" and shape is ROWS_SHAPE:
            block = block.reshape(4, count, BLOCK, PIECE)
        elif axis == "x":
            block = block.reshape(count, 4, BLOCK, PIECE).transpose(1, 0, 2, 3)
        else:
            block = block.reshape(2, count, 2, BLOCK, PIECE).transpose(2, 0, 1, 3, 4)
            block = block.reshape(4, count, BLOCK, PIECE)
        found.append(block)
    return found


def stacked(parts, axis, steps, zs, here, passed=()):
    which = (here[axis] + steps) % 4
    sums = []
    for number, part in enumerate(parts):
        terms = place_block(part, axis, which, zs, here) + [one[number] for one in passed]
        sums.append(add_up(*terms))
    return jnp.stack(sums)


def scatter_places(parts, vectors, ada_part, here):
    axes = (("x", "y"), ("y", "x"))
    passed = []
    for k in range(2):
        axis = axes[k][0]
        low = stacked(parts, axis, 2, (4 * k, 2), here)
        high = stacked(parts, axis, 2, (4 * k + 2, 2), here)
        passed.append((swap(low, axis + "+"), swap(high, axis + "-")))
    for axis, bit in ((0, "z2"), (1, "z1"), (2, "z0")):
        vectors = gather(vectors, bit, here, axis)
    *passed, vectors = tie(*passed, vectors)
    streams = []
    for k in range(2):
        axis = axes[k][0]
        low, high = passed[k]
        halves = ((4 * k, 2), (4 * k + 2, 2))
        ahead = jnp.concatenate(
            [
                stacked(parts, axis, 1, halves[0], here, (low,)),
                stacked(parts, axis, 1, halves[1], here),
            ],
            axis=2,
        )
        back = jnp.concatenate(
            [
                stacked(parts, axis, 3, halves[0], here),
                stacked(parts, axis, 3, halves[1], here, (high,)),
            ],
            axis=2,
        )
        got = (swap(ahead, axis + "+"), swap(back, axis + "-"))
        streams.append(stacked(parts, axis, 0, (4 * k, 4), here, got))
    for axis, bit in ((3, "xh"), (4, "c")):
        vectors = gather(vectors, bit, here, axis)
    streams, vectors = tie(streams, vectors)
    packed = ada_part(vectors)
    sent = []
    for k in range(2):
        axis = axes[k][1]
        for step, move in ((1, "+"), (3, "-"), (2, "2")):
            value = lax.dynamic_index_in_dim(
                streams[k], (here[axis] + step) % 4, 1, keepdims=False
            )
            sent.append((value, axis + move))
    values = tie(*[value for value, _ in sent])
    got = [swap(value, move) for value, (_, move) in zip(values, sent)]
    got = tie(*got)
    results = []
    for k in range(2):
        mine = lax.dynamic_index_in_dim(streams[k], here[axes[k][1]], 1, keepdims=False)
        results.append(add_up(mine, *got[3 * k : 3 * k + 3]))
    return jnp.concatenate(results, axis=1), packed


def scatter_z(values, here):
    number = values.shape[0]
    values = values.reshape(number, 2, 2, 2, BLOCK, PIECE)
    for bit, axis in (("z0", 3), ("z1", 2), ("z2", 1)):
        values = scatter(values, bit, here, axis)
    return values.reshape(number, BLOCK, PIECE)


def gather_pieces(values, here):
    number = values.shape[0]
    values = values.reshape(1, 1, number, BLOCK, PIECE)
    values = gather(values, "xl", here, 1)
    before, after, far = swap(values, "y+"), swap(values, "y-"), swap(values, "y2")
    return jnp.concatenate([values, after, far, before], axis=0).astype(jnp.float32)


def condition_columns(steps, classes, class_table, shard):
    half_width = class_table.shape[1] // 2
    column = BLOCK * shard + jnp.arange(BLOCK)
    place_of = jnp.where(column < half_width, column, column - half_width)
    frequency = jnp.exp(-math.log(10000.0) * place_of.astype(jnp.float32) / half_width)
    angles = steps[:, None] * frequency[None, :]
    time_embed = jnp.where(column[None, :] < half_width, jnp.cos(angles), jnp.sin(angles))
    label_rows = jnp.take(class_table, classes, axis=0)
    label_part = lax.dynamic_slice(label_rows, (0, BLOCK * shard), (label_rows.shape[0], BLOCK))
    return jax.nn.silu(time_embed + label_part.astype(jnp.float32)).astype(jnp.bfloat16)


def local(
    latents,
    cotangent,
    step_ids,
    class_ids,
    class_table,
    rows_weight,
    down_weight,
    bias_weight,
    rows_first,
    down_first,
    bias_first,
    rows_second,
    down_second,
    bias_second,
):
    rep, shard = lax.axis_index("rep"), lax.axis_index("shard")
    here = place(rep, shard)
    width = latents.shape[-1]
    small = jnp.concatenate(
        [
            bias_weight.astype(jnp.bfloat16).astype(jnp.float32),
            step_ids.astype(jnp.float32),
            class_ids.astype(jnp.float32),
            jnp.zeros((22,), jnp.float32),
        ]
    ).reshape(1, 1, 1, 1, 1, -1)
    small = gather(small, "c", here, 4)
    small = gather(small, "xh", here, 3)
    blocks = own_pieces(rows_weight, down_weight, rep).reshape(1, 1, 1, 3, BLOCK, PIECE)
    for axis, bit in ((0, "z2"), (1, "z1"), (2, "z0")):
        blocks, small = tie(blocks, small)
        blocks, small = gather(blocks, bit, here, axis), gather(small, bit, here, axis)
    blocks, small = tie(blocks, small)

    def partial_of(small):
        small = small.reshape(32, -1)
        classes = small[:, 361].astype(jnp.int32)
        columns = condition_columns(small[:, 360], classes, class_table, shard)
        ada_rows = rows_weight[:, : 6 * width].astype(jnp.bfloat16)
        partial = jnp.dot(columns, ada_rows, preferred_element_type=jnp.float32)
        return (partial.reshape(2, 2, 2, 2, 2, -1), columns), small[:, :360].reshape(1, -1)

    (first, second, lower), modulation, biases, cond_columns = gather_weights(
        blocks.reshape(8, 3, BLOCK, PIECE), small, partial_of, here
    )
    first, second = first.reshape(8, 768, PIECE), second.reshape(8, 768, PIECE)
    lower = lower.reshape(2, 3072, PIECE)
    x, dy = latents[0], cotangent[0]
    a1, qkv, lse, o, att, x1, a2 = attention_forward(x, modulation, biases, first)
    output, dx1, datt, expand_grad, lower_grad, hidden_sum, sums = perceptron(
        a2, x1, att, dy, modulation, second, lower, biases
    )
    early = [
        core_swap(expand_grad, ROWS_SHAPE, here)[:2],
        core_swap(lower_grad, DOWN_SHAPE, here)[:2],
    ]
    dqkv, first_grad = attention_backward(datt, qkv, lse, o, a1, first)
    dx, vector = input_backward(
        dqkv, x, dx1, modulation, biases, first, sums, hidden_sum
    )
    early, first_grad, dx, vector = tie(early, first_grad, dx, vector)
    parts = [core_swap(first_grad, ROWS_SHAPE, here)]
    parts.append((*early[0], ROWS_SHAPE))
    parts.append((*early[1], DOWN_SHAPE))
    output, grad_latents = output[None], dx[None]
    vectors = vector.astype(jnp.bfloat16).reshape(1, 1, 1, 1, 1, -1)

    def ada_part(vectors):
        vectors = vectors.reshape(32, -1)
        ada_term = dot_of(cond_columns, vectors[:, : 6 * width], 0, 0)
        bias_sum = jnp.sum(vectors.astype(jnp.float32), axis=0)
        bias_sum = lax.dynamic_slice(bias_sum, (360 * shard,), (360,))
        bias_sum = jnp.pad(bias_sum, (0, 24)).reshape(3, 128).repeat(8, axis=0)
        return jnp.concatenate([ada_term, bias_sum], axis=1).astype(jnp.bfloat16)

    owned, packed = scatter_places(parts, vectors, ada_part, here)
    owned = scatter_z(owned, here)
    for bit in ("xl", "y0", "y1"):
        packed = add_up(packed, swap(packed, bit))
    packed = packed.astype(jnp.float32)
    owned = gather_pieces(owned, here)
    (
        grad_rows,
        new_rows,
        first_rows,
        second_rows,
        grad_down,
        new_down,
        first_down,
        second_down,
    ) = update(
        packed,
        owned,
        rows_weight,
        rows_first,
        rows_second,
        down_weight,
        down_first,
        down_second,
    )
    grad_bias = packed[::8, 6 * width :].reshape(-1)[:360] * (1.0 / 65536)
    new_bias, first_bias, second_bias = adamw(bias_weight, bias_first, bias_second, grad_bias, 0.0)
    return (
        output,
        grad_latents,
        grad_rows,
        grad_down,
        grad_bias,
        new_rows,
        new_down,
        new_bias,
        first_rows,
        first_down,
        first_bias,
        second_rows,
        second_down,
        second_bias,
    )


def solution(mesh):
    placed = (
        P(("rep", "shard"), None, None),
        P(("rep", "shard"), None, None),
        P(("rep", "shard")),
        P(("rep", "shard")),
        P(),
        P("shard", None),
        P("shard", None),
        P("shard"),
        P("shard", None),
        P("shard", None),
        P("shard"),
        P("shard", None),
        P("shard", None),
        P("shard"),
    )
    return jax.shard_map(
        local,
        mesh=mesh,
        in_specs=placed,
        out_specs=(
            P(("rep", "shard"), None, None),
            P(("rep", "shard"), None, None),
            P("shard", None),
            P("shard", None),
            P("shard"),
            P("shard", None),
            P("shard", None),
            P("shard"),
            P("shard", None),
            P("shard", None),
            P("shard"),
            P("shard", None),
            P("shard", None),
            P("shard"),
        ),
        check_vma=False,
    )
```

```python
import math

import jax
import jax.numpy as jnp
from jax import lax
from jax.experimental import pallas as pl
from jax.experimental.pallas import tpu as pltpu
from jax.sharding import PartitionSpec as P

HEAD_FEATURES = 64


norm_eps = 1e-06
gelu_coef = math.sqrt(2.0 / math.pi)
learn_rate = 0.05
beta_one = 0.9
beta_two = 0.95
adam_eps = 1e-08
decay_rate = 0.1
correct_one = 1.0 - 0.9**3
correct_two = 1.0 - 0.95**3


def matmul_result(pattern, first_op, second_op):
    return jnp.einsum(pattern, first_op, second_op, preferred_element_type=jnp.float32)


def normalize(values):
    centred = values - jnp.mean(values, axis=-1, keepdims=True)
    recip = lax.rsqrt(jnp.mean(centred * centred, axis=-1, keepdims=True) + norm_eps)
    return (centred * recip, recip)


def norm_back(grad_normed, normed, recip):
    return recip * (
        grad_normed
        - jnp.mean(grad_normed, axis=-1, keepdims=True)
        - normed * jnp.mean(grad_normed * normed, axis=-1, keepdims=True)
    )


def gelu_pair(preactivation):
    tanh_value = jnp.tanh(
        gelu_coef * (preactivation + 0.044715 * preactivation * preactivation * preactivation)
    )
    result = 0.5 * preactivation * (1.0 + tanh_value)
    slopes = 0.5 * (1.0 + tanh_value) + 0.5 * preactivation * (
        1.0 - tanh_value * tanh_value
    ) * gelu_coef * (1.0 + 3.0 * 0.044715 * preactivation * preactivation)
    return (result, slopes)


def dot_of(left, right, left_axis, right_axis):
    return lax.dot_general(
        left,
        right,
        (((left_axis,), (right_axis,)), ((), ())),
        preferred_element_type=jnp.float32,
    )


def token_sum(values):
    return jnp.sum(values, axis=0, keepdims=True)


ADA_BIAS, QKV_BIAS, ATT_BIAS, HIDDEN_BIAS, DOWN_BIAS = 0, 4608, 6912, 7680, 10752


def mod_row(mod_ref, bias_ref, number):
    cols = slice(768 * number, 768 * (number + 1))
    return mod_ref[:, cols] + bias_ref[:, cols]


def head_masks():
    lane = lax.broadcasted_iota(jnp.int32, (1, 2 * HEAD_FEATURES), 1)
    return [(lane // HEAD_FEATURES == head).astype(jnp.bfloat16) for head in range(2)]


SCORE_SCALE = 1.0 / math.sqrt(HEAD_FEATURES)


def attention_forward_kernel(
    x_ref, mod_ref, bias_ref, weight_ref, a1_ref, qkv_ref, lse_ref, o_ref, att_ref, x1_ref, a2_ref
):
    x = x_ref[...].astype(jnp.float32)
    normed, _ = normalize(x)
    shift, scale = mod_row(mod_ref, bias_ref, 0), mod_row(mod_ref, bias_ref, 1)
    a1_ref[...] = (normed * (1.0 + scale) + shift).astype(jnp.bfloat16)
    for piece in range(6):
        cols = slice(PIECE * piece, PIECE * (piece + 1))
        bias = bias_ref[:, QKV_BIAS + PIECE * piece : QKV_BIAS + PIECE * (piece + 1)]
        product = dot_of(a1_ref[...], weight_ref[piece], 1, 0) + bias
        qkv_ref[:, cols] = product.astype(jnp.bfloat16)
    masks = head_masks()

    def pair(number, carry):
        at_q = pl.ds(pl.multiple_of(number * 128, 128), 128)
        at_k = pl.ds(pl.multiple_of(number * 128 + 768, 128), 128)
        at_v = pl.ds(pl.multiple_of(number * 128 + 1536, 128), 128)
        queries, key_rows, values = qkv_ref[:, at_q], qkv_ref[:, at_k], qkv_ref[:, at_v]
        total = jnp.zeros((256, 128), jnp.float32)
        for head in range(2):
            scores = dot_of(key_rows * masks[head], queries, 1, 1) * SCORE_SCALE
            top = jnp.max(scores, axis=0, keepdims=True)
            lse = top + jnp.log(jnp.sum(jnp.exp(scores - top), axis=0, keepdims=True))
            lse_ref[2 * number + head] = lse
            attend = jnp.exp(scores - lse).astype(jnp.bfloat16)
            total = total + dot_of(attend, values * masks[head], 0, 0)
        o_ref[:, at_q] = total.astype(jnp.bfloat16)
        return carry

    lax.fori_loop(0, 6, pair, 0)
    gate = mod_row(mod_ref, bias_ref, 2)
    for half in range(2):
        cols = slice(PIECE * half, PIECE * (half + 1))
        bias = bias_ref[:, ATT_BIAS + PIECE * half : ATT_BIAS + PIECE * (half + 1)]
        att = dot_of(o_ref[...], weight_ref[6 + half], 1, 0) + bias
        att_ref[:, cols] = att
        x1_ref[:, cols] = x_ref[:, cols].astype(jnp.float32) + gate[:, cols] * att
    normed, _ = normalize(x1_ref[...])
    shift, scale = mod_row(mod_ref, bias_ref, 3), mod_row(mod_ref, bias_ref, 4)
    a2_ref[...] = (normed * (1.0 + scale) + shift).astype(jnp.bfloat16)


def perceptron_kernel(
    a2_ref,
    x1_ref,
    att_ref,
    dy_ref,
    mod_ref,
    expand_ref,
    lower_ref,
    bias_ref,
    out_ref,
    dx1_ref,
    datt_ref,
    expand_grad_ref,
    lower_grad_ref,
    hidden_sum_ref,
    sums_ref,
    g_ref,
    slope_ref,
    dm_ref,
    total_ref,
    turned_ref,
):
    total_ref[...] = jnp.zeros_like(total_ref)
    turned_ref[...] = a2_ref[...].T

    def rise(piece, carry):
        at_bias = pl.ds(pl.multiple_of(HIDDEN_BIAS + piece * PIECE, 128), PIECE)
        hidden = dot_of(a2_ref[...], expand_ref[piece], 1, 0) + bias_ref[:, at_bias]
        value, slope = gelu_pair(hidden)
        value = value.astype(jnp.bfloat16)
        g_ref[piece] = value
        slope_ref[piece] = slope
        rows = pl.ds(pl.multiple_of(piece * PIECE, PIECE), PIECE)
        for half in range(2):
            cols = slice(PIECE * half, PIECE * (half + 1))
            total_ref[:, cols] += dot_of(value, lower_ref[half, rows, :], 1, 0)
        return carry

    lax.fori_loop(0, 8, rise, 0)
    perceptron = total_ref[...] + bias_ref[:, DOWN_BIAS:]
    gate = mod_row(mod_ref, bias_ref, 5)
    dy = dy_ref[...].astype(jnp.float32)
    out_ref[...] = (x1_ref[...] + gate * perceptron).astype(jnp.bfloat16)
    sums_ref[3:4, :] = token_sum(dy * perceptron)
    dm = (dy * gate).astype(jnp.bfloat16)
    dm_ref[...] = dm
    sums_ref[5:6, :] = token_sum(dm.astype(jnp.float32))
    total_ref[...] = jnp.zeros_like(total_ref)

    def fall(piece, carry):
        rows = pl.ds(pl.multiple_of(piece * PIECE, PIECE), PIECE)
        grad = jnp.zeros((256, PIECE), jnp.float32)
        for half in range(2):
            cols = slice(PIECE * half, PIECE * (half + 1))
            grad = grad + dot_of(dm_ref[:, cols], lower_ref[half, rows, :], 1, 1)
        grad = (grad * slope_ref[piece]).astype(jnp.bfloat16)
        hidden_sum_ref[piece] = token_sum(grad.astype(jnp.float32))
        total_ref[...] += dot_of(grad, expand_ref[piece], 1, 1)
        expand_grad_ref[piece] = dot_of(turned_ref[...], grad, 1, 0).astype(jnp.bfloat16)
        for half in range(2):
            cols = slice(PIECE * half, PIECE * (half + 1))
            lower_grad_ref[half, rows, :] = dot_of(g_ref[piece], dm_ref[:, cols], 0, 0).astype(
                jnp.bfloat16
            )
        return carry

    lax.fori_loop(0, 8, fall, 0)
    grad = total_ref[...]
    normed, recip = normalize(x1_ref[...])
    sums_ref[1:2, :] = token_sum(grad)
    sums_ref[2:3, :] = token_sum(grad * normed)
    dx1 = dy_ref[...].astype(jnp.float32) + norm_back(
        grad * (1.0 + mod_row(mod_ref, bias_ref, 4)), normed, recip
    )
    dx1_ref[...] = dx1
    sums_ref[0:1, :] = token_sum(dx1 * att_ref[...])
    datt = (dx1 * mod_row(mod_ref, bias_ref, 2)).astype(jnp.bfloat16)
    datt_ref[...] = datt
    sums_ref[4:5, :] = token_sum(datt.astype(jnp.float32))


def attention_backward_kernel(
    datt_ref, qkv_ref, lse_ref, o_ref, a1_ref, weight_ref, dqkv_ref, grad_ref, do_ref
):
    do_ref[...] = (
        dot_of(datt_ref[:, :PIECE], weight_ref[6], 1, 1)
        + dot_of(datt_ref[:, PIECE:], weight_ref[7], 1, 1)
    ).astype(jnp.bfloat16)
    masks = head_masks()

    def pair(number, carry):
        at_q = pl.ds(pl.multiple_of(number * 128, 128), 128)
        at_k = pl.ds(pl.multiple_of(number * 128 + 768, 128), 128)
        at_v = pl.ds(pl.multiple_of(number * 128 + 1536, 128), 128)
        queries, key_rows, values = qkv_ref[:, at_q], qkv_ref[:, at_k], qkv_ref[:, at_v]
        blend = do_ref[:, at_q]
        dq = jnp.zeros((256, 128), jnp.float32)
        dk = jnp.zeros((256, 128), jnp.float32)
        dv = jnp.zeros((256, 128), jnp.float32)
        for head in range(2):
            keys_here = key_rows * masks[head]
            scores = dot_of(keys_here, queries, 1, 1) * SCORE_SCALE
            attend = jnp.exp(scores - lse_ref[2 * number + head])
            grad = dot_of(values * masks[head], blend, 1, 1)
            delta = jnp.sum(attend * grad, axis=0, keepdims=True)
            ds = (attend * (grad - delta) * SCORE_SCALE).astype(jnp.bfloat16)
            dv = dv + dot_of(attend.astype(jnp.bfloat16), blend * masks[head], 1, 0)
            dk = dk + dot_of(ds, queries * masks[head], 1, 0)
            dq = dq + dot_of(ds, keys_here, 0, 0)
        dqkv_ref[:, at_q] = dq.astype(jnp.bfloat16)
        dqkv_ref[:, at_k] = dk.astype(jnp.bfloat16)
        dqkv_ref[:, at_v] = dv.astype(jnp.bfloat16)
        return carry

    lax.fori_loop(0, 6, pair, 0)
    for piece in range(6):
        cols = slice(PIECE * piece, PIECE * (piece + 1))
        grad_ref[piece] = dot_of(a1_ref[...], dqkv_ref[:, cols], 0, 0).astype(jnp.bfloat16)
    for half in range(2):
        cols = slice(PIECE * half, PIECE * (half + 1))
        grad_ref[6 + half] = dot_of(o_ref[...], datt_ref[:, cols], 0, 0).astype(jnp.bfloat16)


def input_backward_kernel(
    dqkv_ref, x_ref, dx1_ref, mod_ref, bias_ref, weight_ref, sums_ref, hidden_sum_ref, act_ref, dx_ref, vector_ref
):
    grad = jnp.zeros((256, 768), jnp.float32)
    for piece in range(6):
        cols = slice(PIECE * piece, PIECE * (piece + 1))
        grad = grad + dot_of(dqkv_ref[:, cols], weight_ref[piece], 1, 1)
    normed, recip = normalize(x_ref[...].astype(jnp.float32))
    scale = mod_row(mod_ref, bias_ref, 1)
    dx_ref[...] = dx1_ref[...] + norm_back(grad * (1.0 + scale), normed, recip)

    def rounded(row):
        return row.astype(jnp.bfloat16).astype(jnp.float32)

    vector_ref[:, :768] = rounded(token_sum(grad))
    vector_ref[:, 768:1536] = rounded(token_sum(grad * normed))
    for row in range(4):
        vector_ref[:, 1536 + 768 * row : 2304 + 768 * row] = rounded(sums_ref[row : row + 1, :])
    vector_ref[:, QKV_BIAS:ATT_BIAS] = token_sum(dqkv_ref[...].astype(jnp.float32))
    vector_ref[:, ATT_BIAS:HIDDEN_BIAS] = sums_ref[4:5, :]
    for piece in range(8):
        cols = slice(HIDDEN_BIAS + PIECE * piece, HIDDEN_BIAS + PIECE * (piece + 1))
        vector_ref[:, cols] = hidden_sum_ref[piece]
    vector_ref[:, DOWN_BIAS : DOWN_BIAS + 768] = sums_ref[5:6, :]
    vector_ref[:, 11520:12288] = act_ref[...]
    vector_ref[:, 12288:] = jnp.zeros((1, VECTOR - 12288), jnp.float32)


VECTOR = 16384


def adamw_rows(refs, cols, rows, grad):
    weight, first, second, out_grad, new, new_first, new_second = refs
    results = adamw(weight[rows, cols], first[rows, cols], second[rows, cols], grad, decay_rate)
    out_grad[rows, cols] = grad
    new[rows, cols], new_first[rows, cols], new_second[rows, cols] = results


def update_kernel(
    ada_ref,
    owned_ref,
    rows_weight,
    rows_first,
    rows_second,
    down_weight,
    down_first,
    down_second,
    grad_rows,
    new_rows,
    first_rows,
    second_rows,
    grad_down,
    new_down,
    first_down,
    second_down,
):
    factor = 1.0 / 65536
    y = lax.axis_index("rep") // 2
    rows_refs = (
        rows_weight, rows_first, rows_second, grad_rows, new_rows, first_rows, second_rows
    )
    down_refs = (
        down_weight, down_first, down_second, grad_down, new_down, first_down, second_down
    )
    every = slice(0, BLOCK)
    for piece in range(12):
        cols = slice(PIECE * piece, PIECE * (piece + 1))
        adamw_rows(rows_refs, cols, every, ada_ref[:, cols] * factor)
    for piece in range(8):
        place = lax.rem(piece // 2 - y + 4, 4)
        found = [owned_ref[place, piece % 2, part] * factor for part in range(3)]
        cols = slice(4608 + PIECE * piece, 4608 + PIECE * (piece + 1))
        adamw_rows(rows_refs, cols, every, found[0])
        cols = slice(7680 + PIECE * piece, 7680 + PIECE * (piece + 1))
        adamw_rows(rows_refs, cols, every, found[1])
        cols = slice(PIECE * (piece % 2), PIECE * (piece % 2 + 1))
        rows = slice(BLOCK * (piece // 2), BLOCK * (piece // 2 + 1))
        adamw_rows(down_refs, cols, rows, found[2])


def shaped(shape, dtype=jnp.float32):
    return jax.ShapeDtypeStruct(shape, dtype)


def call_kernel(kernel, outs, args, scratch, flops):
    whole = pl.BlockSpec(memory_space=pltpu.VMEM)
    moved = sum(math.prod(value.shape) * value.dtype.itemsize for value in list(args) + list(outs))
    return pl.pallas_call(
        kernel,
        out_shape=outs,
        in_specs=[whole] * len(args),
        out_specs=tuple(whole for _ in outs),
        scratch_shapes=scratch,
        compiler_params=pltpu.CompilerParams(vmem_limit_bytes=52 * 1024 * 1024),
        cost_estimate=pl.CostEstimate(flops=flops, bytes_accessed=moved, transcendentals=0),
    )(*args)


def attention_forward(x, modulation, biases, weight):
    low, wide = jnp.bfloat16, jnp.float32
    outs = (
        shaped((256, 768), low),
        shaped((256, 2304), low),
        shaped((12, 1, 256)),
        shaped((256, 768), low),
        shaped((256, 768)),
        shaped((256, 768)),
        shaped((256, 768), low),
    )
    return call_kernel(
        attention_forward_kernel, outs, (x, modulation, biases, weight), [], 1500000000
    )


def perceptron(a2, x1, att, dy, modulation, expand, lower, biases):
    low = jnp.bfloat16
    outs = (
        shaped((256, 768), low),
        shaped((256, 768)),
        shaped((256, 768), low),
        shaped((8, 768, PIECE), low),
        shaped((2, 3072, PIECE), low),
        shaped((8, 1, PIECE)),
        shaped((8, 768)),
    )
    scratch = [
        pltpu.VMEM((8, 256, PIECE), low),
        pltpu.VMEM((8, 256, PIECE), jnp.float32),
        pltpu.VMEM((256, 768), low),
        pltpu.VMEM((256, 768), jnp.float32),
        pltpu.VMEM((768, 256), low),
    ]
    args = (a2, x1, att, dy, modulation, expand, lower, biases)
    return call_kernel(perceptron_kernel, outs, args, scratch, 7200000000)


def attention_backward(datt, qkv, lse, o, a1, weight):
    low = jnp.bfloat16
    outs = (shaped((256, 2304), low), shaped((8, 768, PIECE), low))
    return call_kernel(
        attention_backward_kernel,
        outs,
        (datt, qkv, lse, o, a1, weight),
        [pltpu.VMEM((256, 768), low)],
        2500000000,
    )


def input_backward(*args):
    outs = (shaped((256, 768)), shaped((1, VECTOR)))
    return call_kernel(input_backward_kernel, outs, args, [], 900000000)


def update(*args):
    outs = tuple(shaped(shape) for shape in 4 * [(BLOCK, 10752)] + 4 * [(96, 768)])
    return call_kernel(update_kernel, outs, args, [], 10000000)


def adamw(weight, first_mom, second_mom, gradient, decay):
    new_first = beta_one * first_mom + (1.0 - beta_one) * gradient
    new_second = beta_two * second_mom + (1.0 - beta_two) * gradient * gradient
    update = new_first / correct_one / (jnp.sqrt(new_second / correct_two) + adam_eps)
    return (weight - learn_rate * (update + decay * weight), new_first, new_second)

def index_of(x, y, z, core):
    return (y * 2 + x % 2) * 32 + z * 4 + (x // 2) * 2 + core


def pairs_of(move):
    pairs = []
    for x in range(4):
        for y in range(4):
            for z in range(8):
                for core in range(2):
                    there = move(x, y, z, core)
                    pairs.append((index_of(x, y, z, core), index_of(*there)))
    return pairs


MOVES = {
    "c": pairs_of(lambda x, y, z, core: (x, y, z, 1 - core)),
    "xh": pairs_of(lambda x, y, z, core: (3 - x, y, z, core)),
    "xl": pairs_of(lambda x, y, z, core: (x ^ 1, y, z, core)),
    "y0": pairs_of(lambda x, y, z, core: (x, y ^ 1, z, core)),
    "y1": pairs_of(lambda x, y, z, core: (x, 3 - y, z, core)),
    "z0": pairs_of(lambda x, y, z, core: (x, y, z ^ 1, core)),
    "z1": pairs_of(lambda x, y, z, core: (x, y, z ^ 2, core)),
    "z2": pairs_of(lambda x, y, z, core: (x, y, z ^ 4, core)),
    "x+": pairs_of(lambda x, y, z, core: ((x + 1) % 4, y, z, core)),
    "x-": pairs_of(lambda x, y, z, core: ((x + 3) % 4, y, z, core)),
    "y+": pairs_of(lambda x, y, z, core: (x, (y + 1) % 4, z, core)),
    "x2": pairs_of(lambda x, y, z, core: (x ^ 2, y, z, core)),
    "y2": pairs_of(lambda x, y, z, core: (x, y ^ 2, z, core)),
    "y-": pairs_of(lambda x, y, z, core: (x, (y + 3) % 4, z, core)),
}
BLOCK = 24
PIECE = 384


def place(rep, shard):
    y, xl = rep >> 1, rep & 1
    z, xh, c = shard >> 2, (shard >> 1) & 1, shard & 1
    return {
        "z2": z >> 2,
        "z1": (z >> 1) & 1,
        "z0": z & 1,
        "xh": xh,
        "c": c,
        "xl": xl,
        "y0": y & 1,
        "y1": y >> 1,
        "x": xh * 2 + xl,
        "y": y,
    }


def swap(values, move):
    return lax.ppermute(values, ("rep", "shard"), MOVES[move])


def tie(*values):
    return lax.optimization_barrier(values)


def join(mine, theirs, here, axis):
    low = jnp.where(here == 0, mine, theirs)
    high = jnp.where(here == 0, theirs, mine)
    return jnp.concatenate([low, high], axis=axis)


def gather(values, bit, here, axis):
    return join(values, swap(values, bit), here[bit], axis)


def take_half(values, which, axis):
    half = values.shape[axis] // 2
    return lax.dynamic_slice_in_dim(values, which * half, half, axis)


def add_up(*terms):
    total = terms[0].astype(jnp.float32)
    for term in terms[1:]:
        total = total + term.astype(jnp.float32)
    return total.astype(terms[0].dtype)


def scatter(values, bit, here, axis):
    sent = take_half(values, 1 - here[bit], axis)
    kept = take_half(values, here[bit], axis)
    return add_up(kept, swap(sent, bit))


def assemble_kernel(*refs):
    inputs, (first, second, down), sems = refs[:20], refs[20:23], refs[23]
    rep, shard = lax.axis_index("rep"), lax.axis_index("shard")
    y, x = rep // 2, ((shard // 2) % 2) * 2 + rep % 2
    c = shard % 2
    steps = (0, 1, 3, 2, 2)
    for stream in range(2):
        for side in range(2):
            core = c if side == 0 else 1 - c
            for kind in range(5):
                ref = inputs[(stream * 2 + side) * 5 + kind]
                z_start = 4 * stream + (2 if kind == 4 else 0)
                z_count = 2 if kind >= 3 else 4
                for other in range(4):
                    ahead, inner = steps[kind], (0, 1, 2, 3)[other]
                    x_at = (x + (inner if stream == 0 else ahead)) % 4
                    y_at = (y + (ahead if stream == 0 else inner)) % 4
                    xh, xl = x_at // 2, x_at % 2
                    zs = pl.ds(z_start, z_count)
                    for part in range(3):
                        if part == 2:
                            target = down.at[xl, zs, xh, core, y_at]
                        else:
                            target = (first, second)[part].at[y_at, xl, zs, xh, core]
                        pltpu.make_async_copy(ref.at[other, part], target, sems.at[part]).start()
    for part, out in enumerate((first, second, down)):
        pltpu.make_async_copy(out, out, sems.at[part]).wait()


def assemble(pieces):
    shape = jax.ShapeDtypeStruct((4, 2, 8, 2, 2, BLOCK, PIECE), jnp.bfloat16)
    down = jax.ShapeDtypeStruct((2, 8, 2, 2, 4, BLOCK, PIECE), jnp.bfloat16)
    return pl.pallas_call(
        assemble_kernel,
        out_shape=(shape, shape, down),
        in_specs=[pl.BlockSpec(memory_space=pl.ANY)] * 20,
        out_specs=[pl.BlockSpec(memory_space=pltpu.VMEM)] * 3,
        scratch_shapes=[pltpu.SemaphoreType.DMA((3,))],
        compiler_params=pltpu.CompilerParams(vmem_limit_bytes=48 * 1024 * 1024),
        cost_estimate=pl.CostEstimate(flops=0, bytes_accessed=30000000, transcendentals=0),
    )(*pieces)


def own_pieces(rows_weight, down_weight, rep):
    return jnp.stack(
        [
            lax.dynamic_slice(rows_weight, (0, 4608 + PIECE * rep), (BLOCK, PIECE)),
            lax.dynamic_slice(rows_weight, (0, 7680 + PIECE * rep), (BLOCK, PIECE)),
            lax.dynamic_slice(
                down_weight, (BLOCK * (rep >> 1), PIECE * (rep & 1)), (BLOCK, PIECE)
            ),
        ]
    ).astype(jnp.bfloat16)


def ring_round_one(block, axis):
    return swap(block, axis + "+"), swap(block, axis + "-")


def ring_round_two(before, after, axis, cut_axis):
    half = before.shape[cut_axis] // 2
    low = lax.slice_in_dim(before, 0, half, axis=cut_axis)
    high = lax.slice_in_dim(after, half, 2 * half, axis=cut_axis)
    return swap(low, axis + "+"), swap(high, axis + "-")


def gather_weights(values, small, partial_of, here):
    blocks = [values[4 * k : 4 * k + 4].transpose(1, 0, 2, 3)[None] for k in range(2)]
    first_axes, last_axes = ("x", "y"), ("y", "x")
    direct = [[swap(blocks[k], first_axes[k] + step) for step in ("-", "2", "+")] for k in range(2)]
    direct, small = tie(direct, small)
    blocks = [
        jnp.concatenate([blocks[k]] + direct[k], axis=0) for k in range(2)
    ]
    near = [ring_round_one(blocks[k], last_axes[k]) for k in range(2)]
    partial = partial_of(small)
    biases = gather(gather(small, "xh", here, 3), "c", here, 4)
    partial = scatter(partial, "z0", here, 2)
    near, partial, biases = tie(near, partial, biases)
    far = [ring_round_two(*near[k], last_axes[k], 2) for k in range(2)]
    for bit, axis in (("z1", 1), ("z2", 0)):
        partial = scatter(partial, bit, here, axis)
    pieces = []
    for k in range(2):
        mine = [blocks[k], near[k][1], near[k][0], far[k][0], far[k][1]]
        pieces += mine + [swap(piece, "c") for piece in mine]
    biases = biases.reshape(32, -1)[:, :360].reshape(1, -1)
    return assemble(pieces), partial.reshape(1, -1), biases


ROWS_SHAPE = (4, 2, 8, 2, 2, BLOCK, PIECE)
DOWN_SHAPE = (2, 8, 2, 2, 4, BLOCK, PIECE)


def core_swap(gradient, shape, here):
    gradient = gradient.reshape(shape)
    axis = 4 if shape is ROWS_SHAPE else 3
    sent = lax.dynamic_index_in_dim(gradient, 1 - here["c"], axis, keepdims=True)
    return gradient, swap(sent, "c"), shape


def place_block(part, axis, which, zs, here):
    whole, received, shape = part
    first, count = zs
    xh, xl = which // 2, which % 2
    found = []
    for values, core in ((whole, here["c"]), (received, 0)):
        if axis == "x":
            if shape is ROWS_SHAPE:
                start, size = (0, xl, first, xh, core, 0, 0), (4, 1, count, 1, 1, BLOCK, PIECE)
            else:
                start, size = (xl, first, xh, core, 0, 0, 0), (1, count, 1, 1, 4, BLOCK, PIECE)
        elif shape is ROWS_SHAPE:
            start, size = (which, 0, first, 0, core, 0, 0), (1, 2, count, 2, 1, BLOCK, PIECE)
        else:
            start, size = (0, first, 0, core, which, 0, 0), (2, count, 2, 1, 1, BLOCK, PIECE)
        block = lax.dynamic_slice(values, start, size)
        if axis == "x" and shape is ROWS_SHAPE:
            block = block.reshape(4, count, BLOCK, PIECE)
        elif axis == "x":
            block = block.reshape(count, 4, BLOCK, PIECE).transpose(1, 0, 2, 3)
        else:
            block = block.reshape(2, count, 2, BLOCK, PIECE).transpose(2, 0, 1, 3, 4)
            block = block.reshape(4, count, BLOCK, PIECE)
        found.append(block)
    return found


def stacked(parts, axis, steps, zs, here, passed=()):
    which = (here[axis] + steps) % 4
    sums = []
    for number, part in enumerate(parts):
        terms = place_block(part, axis, which, zs, here) + [one[number] for one in passed]
        sums.append(add_up(*terms))
    return jnp.stack(sums)


def scatter_places(parts, vectors, ada_part, here):
    axes = (("x", "y"), ("y", "x"))
    passed = []
    for k in range(2):
        axis = axes[k][0]
        low = stacked(parts, axis, 2, (4 * k, 2), here)
        high = stacked(parts, axis, 2, (4 * k + 2, 2), here)
        passed.append((swap(low, axis + "+"), swap(high, axis + "-")))
    passed = tie(*passed)
    streams = []
    for k in range(2):
        axis = axes[k][0]
        low, high = passed[k]
        halves = ((4 * k, 2), (4 * k + 2, 2))
        ahead = jnp.concatenate(
            [
                stacked(parts, axis, 1, halves[0], here, (low,)),
                stacked(parts, axis, 1, halves[1], here),
            ],
            axis=2,
        )
        back = jnp.concatenate(
            [
                stacked(parts, axis, 3, halves[0], here),
                stacked(parts, axis, 3, halves[1], here, (high,)),
            ],
            axis=2,
        )
        got = (swap(ahead, axis + "+"), swap(back, axis + "-"))
        streams.append(stacked(parts, axis, 0, (4 * k, 4), here, got))
    sent = []
    for k in range(2):
        axis = axes[k][1]
        for step, move in ((1, "+"), (3, "-"), (2, "2")):
            value = lax.dynamic_index_in_dim(
                streams[k], (here[axis] + step) % 4, 1, keepdims=False
            )
            sent.append((value, axis + move))
    values = tie(*[value for value, _ in sent])
    got = [swap(value, move) for value, (_, move) in zip(values, sent)]
    *got, vectors = tie(*got, vectors)
    packed = ada_part(vectors)
    results = []
    for k in range(2):
        mine = lax.dynamic_index_in_dim(streams[k], here[axes[k][1]], 1, keepdims=False)
        results.append(add_up(mine, *got[3 * k : 3 * k + 3]))
    return jnp.concatenate(results, axis=1), packed


def scatter_z(values, here):
    number = values.shape[0]
    values = values.reshape(number, 2, 2, 2, BLOCK, PIECE)
    for bit, axis in (("z0", 3), ("z1", 2), ("z2", 1)):
        values = scatter(values, bit, here, axis)
    return values.reshape(number, BLOCK, PIECE)


def gather_pieces(values, here):
    number = values.shape[0]
    values = values.reshape(1, 1, number, BLOCK, PIECE)
    values = gather(values, "xl", here, 1)
    before, after, far = swap(values, "y+"), swap(values, "y-"), swap(values, "y2")
    return jnp.concatenate([values, after, far, before], axis=0).astype(jnp.float32)


def condition(steps, classes, class_table, first, count):
    half_width = class_table.shape[1] // 2
    column = first + jnp.arange(count)
    place_of = jnp.where(column < half_width, column, column - half_width)
    frequency = jnp.exp(-math.log(10000.0) * place_of.astype(jnp.float32) / half_width)
    angles = steps.astype(jnp.float32)[:, None] * frequency[None, :]
    time_embed = jnp.where(column[None, :] < half_width, jnp.cos(angles), jnp.sin(angles))
    label_rows = jnp.take(class_table, classes, axis=0)
    label_part = lax.dynamic_slice(label_rows, (0, first), (label_rows.shape[0], count))
    return jax.nn.silu(time_embed + label_part.astype(jnp.float32)).astype(jnp.bfloat16)


def local(
    latents,
    cotangent,
    step_ids,
    class_ids,
    class_table,
    rows_weight,
    down_weight,
    bias_weight,
    rows_first,
    down_first,
    bias_first,
    rows_second,
    down_second,
    bias_second,
):
    rep, shard = lax.axis_index("rep"), lax.axis_index("shard")
    here = place(rep, shard)
    width = latents.shape[-1]
    small = jnp.concatenate(
        [
            bias_weight.astype(jnp.bfloat16).astype(jnp.float32),
            step_ids.astype(jnp.float32),
            class_ids.astype(jnp.float32),
            jnp.zeros((22,), jnp.float32),
        ]
    ).reshape(1, 1, 1, 1, 1, -1)
    ada_rows = rows_weight[:, : 6 * width].astype(jnp.bfloat16).reshape(1, 1, BLOCK, 6 * width)
    blocks = own_pieces(rows_weight, down_weight, rep).reshape(1, 1, 1, 3, BLOCK, PIECE)
    ada_rows = gather(ada_rows, "xh", here, 0)
    for axis, bit in ((0, "z2"), (1, "z1"), (2, "z0")):
        blocks, small = tie(blocks, small)
        blocks, small = gather(blocks, bit, here, axis), gather(small, bit, here, axis)
        if bit == "z1":
            ada_rows = gather(ada_rows, "c", here, 1)
    blocks, small, ada_rows = tie(blocks, small, ada_rows)

    def partial_of(small):
        small = small.reshape(8, -1)
        classes = small[:, 361].astype(jnp.int32)
        columns = condition(small[:, 360], classes, class_table, 96 * (shard // 4), 96)
        partial = jnp.dot(
            columns, ada_rows.reshape(96, 6 * width), preferred_element_type=jnp.float32
        )
        return partial.reshape(2, 2, 2, 1, 1, -1)

    (first, second, lower), modulation, biases = gather_weights(
        blocks.reshape(8, 3, BLOCK, PIECE), small, partial_of, here
    )
    first, second = first.reshape(8, 768, PIECE), second.reshape(8, 768, PIECE)
    lower = lower.reshape(2, 3072, PIECE)
    cond_act = condition(step_ids, class_ids, class_table, 0, width).astype(jnp.float32)
    x, dy = latents[0], cotangent[0]
    a1, qkv, lse, o, att, x1, a2 = attention_forward(x, modulation, biases, first)
    output, dx1, datt, expand_grad, lower_grad, hidden_sum, sums = perceptron(
        a2, x1, att, dy, modulation, second, lower, biases
    )
    early = [
        core_swap(expand_grad, ROWS_SHAPE, here)[:2],
        core_swap(lower_grad, DOWN_SHAPE, here)[:2],
    ]
    dqkv, first_grad = attention_backward(datt, qkv, lse, o, a1, first)
    dx, vector = input_backward(
        dqkv, x, dx1, modulation, biases, first, sums, hidden_sum, cond_act
    )
    early, first_grad, dx, vector = tie(early, first_grad, dx, vector)
    parts = [core_swap(first_grad, ROWS_SHAPE, here)]
    parts.append((*early[0], ROWS_SHAPE))
    parts.append((*early[1], DOWN_SHAPE))
    output, grad_latents = output[None], dx[None]
    vectors = lax.all_gather(vector, "shard", axis=0, tiled=True)

    def ada_part(vectors):
        dmod = vectors[:, : 6 * width].astype(jnp.bfloat16)
        columns = lax.dynamic_slice(vectors, (0, 15 * width + BLOCK * shard), (32, BLOCK))
        ada_term = dot_of(columns.astype(jnp.bfloat16), dmod, 0, 0)
        bias_sum = jnp.sum(vectors[:, : 15 * width], axis=0)
        bias_sum = lax.dynamic_slice(bias_sum, (360 * shard,), (360,))
        bias_sum = jnp.pad(bias_sum, (0, 24)).reshape(3, 128).repeat(8, axis=0)
        return jnp.concatenate([ada_term, bias_sum], axis=1).astype(jnp.bfloat16)

    owned, packed = scatter_places(parts, vectors, ada_part, here)
    owned = scatter_z(owned, here)
    for bit in ("xl", "y0", "y1"):
        packed = add_up(packed, swap(packed, bit))
    packed = packed.astype(jnp.float32)
    owned = gather_pieces(owned, here)
    (
        grad_rows,
        new_rows,
        first_rows,
        second_rows,
        grad_down,
        new_down,
        first_down,
        second_down,
    ) = update(
        packed,
        owned,
        rows_weight,
        rows_first,
        rows_second,
        down_weight,
        down_first,
        down_second,
    )
    grad_bias = packed[::8, 6 * width :].reshape(-1)[:360] * (1.0 / 65536)
    new_bias, first_bias, second_bias = adamw(bias_weight, bias_first, bias_second, grad_bias, 0.0)
    return (
        output,
        grad_latents,
        grad_rows,
        grad_down,
        grad_bias,
        new_rows,
        new_down,
        new_bias,
        first_rows,
        first_down,
        first_bias,
        second_rows,
        second_down,
        second_bias,
    )


def solution(mesh):
    placed = (
        P(("rep", "shard"), None, None),
        P(("rep", "shard"), None, None),
        P(("rep", "shard")),
        P(("rep", "shard")),
        P(),
        P("shard", None),
        P("shard", None),
        P("shard"),
        P("shard", None),
        P("shard", None),
        P("shard"),
        P("shard", None),
        P("shard", None),
        P("shard"),
    )
    return jax.shard_map(
        local,
        mesh=mesh,
        in_specs=placed,
        out_specs=(
            P(("rep", "shard"), None, None),
            P(("rep", "shard"), None, None),
            P("shard", None),
            P("shard", None),
            P("shard"),
            P("shard", None),
            P("shard", None),
            P("shard"),
            P("shard", None),
            P("shard", None),
            P("shard"),
            P("shard", None),
            P("shard", None),
            P("shard"),
        ),
        check_vma=False,
    )
```

```python
import math

import jax
import jax.numpy as jnp
from jax import lax
from jax.experimental import pallas as pl
from jax.experimental.pallas import tpu as pltpu
from jax.sharding import PartitionSpec as P

HEAD_FEATURES = 64


norm_eps = 1e-06
gelu_coef = math.sqrt(2.0 / math.pi)
learn_rate = 0.05
beta_one = 0.9
beta_two = 0.95
adam_eps = 1e-08
decay_rate = 0.1
correct_one = 1.0 - 0.9**3
correct_two = 1.0 - 0.95**3


def matmul_result(pattern, first_op, second_op):
    return jnp.einsum(pattern, first_op, second_op, preferred_element_type=jnp.float32)


def normalize(values):
    centred = values - jnp.mean(values, axis=-1, keepdims=True)
    recip = lax.rsqrt(jnp.mean(centred * centred, axis=-1, keepdims=True) + norm_eps)
    return (centred * recip, recip)


def norm_back(grad_normed, normed, recip):
    return recip * (
        grad_normed
        - jnp.mean(grad_normed, axis=-1, keepdims=True)
        - normed * jnp.mean(grad_normed * normed, axis=-1, keepdims=True)
    )


def gelu_pair(preactivation):
    tanh_value = jnp.tanh(
        gelu_coef * (preactivation + 0.044715 * preactivation * preactivation * preactivation)
    )
    result = 0.5 * preactivation * (1.0 + tanh_value)
    slopes = 0.5 * (1.0 + tanh_value) + 0.5 * preactivation * (
        1.0 - tanh_value * tanh_value
    ) * gelu_coef * (1.0 + 3.0 * 0.044715 * preactivation * preactivation)
    return (result, slopes)


def dot_of(left, right, left_axis, right_axis):
    return lax.dot_general(
        left,
        right,
        (((left_axis,), (right_axis,)), ((), ())),
        preferred_element_type=jnp.float32,
    )


def token_sum(values):
    return jnp.sum(values, axis=0, keepdims=True)


ADA_BIAS, QKV_BIAS, ATT_BIAS, HIDDEN_BIAS, DOWN_BIAS = 0, 4608, 6912, 7680, 10752


def mod_row(mod_ref, bias_ref, number):
    cols = slice(768 * number, 768 * (number + 1))
    return mod_ref[:, cols] + bias_ref[:, cols]


def head_masks():
    lane = lax.broadcasted_iota(jnp.int32, (1, 2 * HEAD_FEATURES), 1)
    return [(lane // HEAD_FEATURES == head).astype(jnp.bfloat16) for head in range(2)]


SCORE_SCALE = 1.0 / math.sqrt(HEAD_FEATURES)


def attention_forward_kernel(
    x_ref, mod_ref, bias_ref, weight_ref, a1_ref, qkv_ref, lse_ref, o_ref, att_ref, x1_ref, a2_ref
):
    x = x_ref[...].astype(jnp.float32)
    normed, _ = normalize(x)
    shift, scale = mod_row(mod_ref, bias_ref, 0), mod_row(mod_ref, bias_ref, 1)
    a1_ref[...] = (normed * (1.0 + scale) + shift).astype(jnp.bfloat16)
    for piece in range(6):
        cols = slice(PIECE * piece, PIECE * (piece + 1))
        bias = bias_ref[:, QKV_BIAS + PIECE * piece : QKV_BIAS + PIECE * (piece + 1)]
        product = dot_of(a1_ref[...], weight_ref[piece], 1, 0) + bias
        qkv_ref[:, cols] = product.astype(jnp.bfloat16)
    masks = head_masks()

    def pair(number, carry):
        at_q = pl.ds(pl.multiple_of(number * 128, 128), 128)
        at_k = pl.ds(pl.multiple_of(number * 128 + 768, 128), 128)
        at_v = pl.ds(pl.multiple_of(number * 128 + 1536, 128), 128)
        queries, key_rows, values = qkv_ref[:, at_q], qkv_ref[:, at_k], qkv_ref[:, at_v]
        total = jnp.zeros((256, 128), jnp.float32)
        for head in range(2):
            scores = dot_of(key_rows * masks[head], queries, 1, 1) * SCORE_SCALE
            top = jnp.max(scores, axis=0, keepdims=True)
            lse = top + jnp.log(jnp.sum(jnp.exp(scores - top), axis=0, keepdims=True))
            lse_ref[2 * number + head] = lse
            attend = jnp.exp(scores - lse).astype(jnp.bfloat16)
            total = total + dot_of(attend, values * masks[head], 0, 0)
        o_ref[:, at_q] = total.astype(jnp.bfloat16)
        return carry

    lax.fori_loop(0, 6, pair, 0)
    gate = mod_row(mod_ref, bias_ref, 2)
    for half in range(2):
        cols = slice(PIECE * half, PIECE * (half + 1))
        bias = bias_ref[:, ATT_BIAS + PIECE * half : ATT_BIAS + PIECE * (half + 1)]
        att = dot_of(o_ref[...], weight_ref[6 + half], 1, 0) + bias
        att_ref[:, cols] = att
        x1_ref[:, cols] = x_ref[:, cols].astype(jnp.float32) + gate[:, cols] * att
    normed, _ = normalize(x1_ref[...])
    shift, scale = mod_row(mod_ref, bias_ref, 3), mod_row(mod_ref, bias_ref, 4)
    a2_ref[...] = (normed * (1.0 + scale) + shift).astype(jnp.bfloat16)


def perceptron_kernel(
    a2_ref,
    x1_ref,
    att_ref,
    dy_ref,
    mod_ref,
    expand_ref,
    lower_ref,
    bias_ref,
    out_ref,
    dx1_ref,
    datt_ref,
    expand_grad_ref,
    lower_grad_ref,
    hidden_sum_ref,
    sums_ref,
    g_ref,
    slope_ref,
    dm_ref,
    total_ref,
    turned_ref,
):
    total_ref[...] = jnp.zeros_like(total_ref)
    turned_ref[...] = a2_ref[...].T

    def rise(piece, carry):
        at_bias = pl.ds(pl.multiple_of(HIDDEN_BIAS + piece * PIECE, 128), PIECE)
        hidden = dot_of(a2_ref[...], expand_ref[piece], 1, 0) + bias_ref[:, at_bias]
        value, slope = gelu_pair(hidden)
        value = value.astype(jnp.bfloat16)
        g_ref[piece] = value
        slope_ref[piece] = slope
        rows = pl.ds(pl.multiple_of(piece * PIECE, PIECE), PIECE)
        for half in range(2):
            cols = slice(PIECE * half, PIECE * (half + 1))
            total_ref[:, cols] += dot_of(value, lower_ref[half, rows, :], 1, 0)
        return carry

    lax.fori_loop(0, 8, rise, 0)
    perceptron = total_ref[...] + bias_ref[:, DOWN_BIAS:]
    gate = mod_row(mod_ref, bias_ref, 5)
    dy = dy_ref[...].astype(jnp.float32)
    out_ref[...] = (x1_ref[...] + gate * perceptron).astype(jnp.bfloat16)
    sums_ref[3:4, :] = token_sum(dy * perceptron)
    dm = (dy * gate).astype(jnp.bfloat16)
    dm_ref[...] = dm
    sums_ref[5:6, :] = token_sum(dm.astype(jnp.float32))
    total_ref[...] = jnp.zeros_like(total_ref)

    def fall(piece, carry):
        rows = pl.ds(pl.multiple_of(piece * PIECE, PIECE), PIECE)
        grad = jnp.zeros((256, PIECE), jnp.float32)
        for half in range(2):
            cols = slice(PIECE * half, PIECE * (half + 1))
            grad = grad + dot_of(dm_ref[:, cols], lower_ref[half, rows, :], 1, 1)
        grad = (grad * slope_ref[piece]).astype(jnp.bfloat16)
        hidden_sum_ref[piece] = token_sum(grad.astype(jnp.float32))
        total_ref[...] += dot_of(grad, expand_ref[piece], 1, 1)
        expand_grad_ref[piece] = dot_of(turned_ref[...], grad, 1, 0).astype(jnp.bfloat16)
        for half in range(2):
            cols = slice(PIECE * half, PIECE * (half + 1))
            lower_grad_ref[half, rows, :] = dot_of(g_ref[piece], dm_ref[:, cols], 0, 0).astype(
                jnp.bfloat16
            )
        return carry

    lax.fori_loop(0, 8, fall, 0)
    grad = total_ref[...]
    normed, recip = normalize(x1_ref[...])
    sums_ref[1:2, :] = token_sum(grad)
    sums_ref[2:3, :] = token_sum(grad * normed)
    dx1 = dy_ref[...].astype(jnp.float32) + norm_back(
        grad * (1.0 + mod_row(mod_ref, bias_ref, 4)), normed, recip
    )
    dx1_ref[...] = dx1
    sums_ref[0:1, :] = token_sum(dx1 * att_ref[...])
    datt = (dx1 * mod_row(mod_ref, bias_ref, 2)).astype(jnp.bfloat16)
    datt_ref[...] = datt
    sums_ref[4:5, :] = token_sum(datt.astype(jnp.float32))


def attention_backward_kernel(
    datt_ref, qkv_ref, lse_ref, o_ref, a1_ref, weight_ref, dqkv_ref, grad_ref, do_ref
):
    do_ref[...] = (
        dot_of(datt_ref[:, :PIECE], weight_ref[6], 1, 1)
        + dot_of(datt_ref[:, PIECE:], weight_ref[7], 1, 1)
    ).astype(jnp.bfloat16)
    masks = head_masks()

    def pair(number, carry):
        at_q = pl.ds(pl.multiple_of(number * 128, 128), 128)
        at_k = pl.ds(pl.multiple_of(number * 128 + 768, 128), 128)
        at_v = pl.ds(pl.multiple_of(number * 128 + 1536, 128), 128)
        queries, key_rows, values = qkv_ref[:, at_q], qkv_ref[:, at_k], qkv_ref[:, at_v]
        blend = do_ref[:, at_q]
        dq = jnp.zeros((256, 128), jnp.float32)
        dk = jnp.zeros((256, 128), jnp.float32)
        dv = jnp.zeros((256, 128), jnp.float32)
        for head in range(2):
            keys_here = key_rows * masks[head]
            scores = dot_of(keys_here, queries, 1, 1) * SCORE_SCALE
            attend = jnp.exp(scores - lse_ref[2 * number + head])
            grad = dot_of(values * masks[head], blend, 1, 1)
            delta = jnp.sum(attend * grad, axis=0, keepdims=True)
            ds = (attend * (grad - delta) * SCORE_SCALE).astype(jnp.bfloat16)
            dv = dv + dot_of(attend.astype(jnp.bfloat16), blend * masks[head], 1, 0)
            dk = dk + dot_of(ds, queries * masks[head], 1, 0)
            dq = dq + dot_of(ds, keys_here, 0, 0)
        dqkv_ref[:, at_q] = dq.astype(jnp.bfloat16)
        dqkv_ref[:, at_k] = dk.astype(jnp.bfloat16)
        dqkv_ref[:, at_v] = dv.astype(jnp.bfloat16)
        return carry

    lax.fori_loop(0, 6, pair, 0)
    for piece in range(6):
        cols = slice(PIECE * piece, PIECE * (piece + 1))
        grad_ref[piece] = dot_of(a1_ref[...], dqkv_ref[:, cols], 0, 0).astype(jnp.bfloat16)
    for half in range(2):
        cols = slice(PIECE * half, PIECE * (half + 1))
        grad_ref[6 + half] = dot_of(o_ref[...], datt_ref[:, cols], 0, 0).astype(jnp.bfloat16)


def input_backward_kernel(
    dqkv_ref, x_ref, dx1_ref, mod_ref, bias_ref, weight_ref, sums_ref, hidden_sum_ref, act_ref, dx_ref, vector_ref
):
    grad = jnp.zeros((256, 768), jnp.float32)
    for piece in range(6):
        cols = slice(PIECE * piece, PIECE * (piece + 1))
        grad = grad + dot_of(dqkv_ref[:, cols], weight_ref[piece], 1, 1)
    normed, recip = normalize(x_ref[...].astype(jnp.float32))
    scale = mod_row(mod_ref, bias_ref, 1)
    dx_ref[...] = dx1_ref[...] + norm_back(grad * (1.0 + scale), normed, recip)

    def rounded(row):
        return row.astype(jnp.bfloat16).astype(jnp.float32)

    vector_ref[:, :768] = rounded(token_sum(grad))
    vector_ref[:, 768:1536] = rounded(token_sum(grad * normed))
    for row in range(4):
        vector_ref[:, 1536 + 768 * row : 2304 + 768 * row] = rounded(sums_ref[row : row + 1, :])
    vector_ref[:, QKV_BIAS:ATT_BIAS] = token_sum(dqkv_ref[...].astype(jnp.float32))
    vector_ref[:, ATT_BIAS:HIDDEN_BIAS] = sums_ref[4:5, :]
    for piece in range(8):
        cols = slice(HIDDEN_BIAS + PIECE * piece, HIDDEN_BIAS + PIECE * (piece + 1))
        vector_ref[:, cols] = hidden_sum_ref[piece]
    vector_ref[:, DOWN_BIAS : DOWN_BIAS + 768] = sums_ref[5:6, :]
    vector_ref[:, 11520:12288] = act_ref[...]


VECTOR = 12288


def adamw_rows(refs, cols, rows, grad):
    weight, first, second, out_grad, new, new_first, new_second = refs
    results = adamw(weight[rows, cols], first[rows, cols], second[rows, cols], grad, decay_rate)
    out_grad[rows, cols] = grad
    new[rows, cols], new_first[rows, cols], new_second[rows, cols] = results


def update_kernel(
    ada_ref,
    owned_ref,
    rows_weight,
    rows_first,
    rows_second,
    down_weight,
    down_first,
    down_second,
    grad_rows,
    new_rows,
    first_rows,
    second_rows,
    grad_down,
    new_down,
    first_down,
    second_down,
):
    factor = 1.0 / 65536
    y = lax.axis_index("rep") // 2
    rows_refs = (
        rows_weight, rows_first, rows_second, grad_rows, new_rows, first_rows, second_rows
    )
    down_refs = (
        down_weight, down_first, down_second, grad_down, new_down, first_down, second_down
    )
    every = slice(0, BLOCK)
    for piece in range(12):
        cols = slice(PIECE * piece, PIECE * (piece + 1))
        adamw_rows(rows_refs, cols, every, ada_ref[:, cols] * factor)
    for piece in range(8):
        place = lax.rem(piece // 2 - y + 4, 4)
        found = [owned_ref[place, piece % 2, part] * factor for part in range(3)]
        cols = slice(4608 + PIECE * piece, 4608 + PIECE * (piece + 1))
        adamw_rows(rows_refs, cols, every, found[0])
        cols = slice(7680 + PIECE * piece, 7680 + PIECE * (piece + 1))
        adamw_rows(rows_refs, cols, every, found[1])
        cols = slice(PIECE * (piece % 2), PIECE * (piece % 2 + 1))
        rows = slice(BLOCK * (piece // 2), BLOCK * (piece // 2 + 1))
        adamw_rows(down_refs, cols, rows, found[2])


def shaped(shape, dtype=jnp.float32):
    return jax.ShapeDtypeStruct(shape, dtype)


def call_kernel(kernel, outs, args, scratch, flops):
    whole = pl.BlockSpec(memory_space=pltpu.VMEM)
    moved = sum(math.prod(value.shape) * value.dtype.itemsize for value in list(args) + list(outs))
    return pl.pallas_call(
        kernel,
        out_shape=outs,
        in_specs=[whole] * len(args),
        out_specs=tuple(whole for _ in outs),
        scratch_shapes=scratch,
        compiler_params=pltpu.CompilerParams(vmem_limit_bytes=52 * 1024 * 1024),
        cost_estimate=pl.CostEstimate(flops=flops, bytes_accessed=moved, transcendentals=0),
    )(*args)


def attention_forward(x, modulation, biases, weight):
    low, wide = jnp.bfloat16, jnp.float32
    outs = (
        shaped((256, 768), low),
        shaped((256, 2304), low),
        shaped((12, 1, 256)),
        shaped((256, 768), low),
        shaped((256, 768)),
        shaped((256, 768)),
        shaped((256, 768), low),
    )
    return call_kernel(
        attention_forward_kernel, outs, (x, modulation, biases, weight), [], 1500000000
    )


def perceptron(a2, x1, att, dy, modulation, expand, lower, biases):
    low = jnp.bfloat16
    outs = (
        shaped((256, 768), low),
        shaped((256, 768)),
        shaped((256, 768), low),
        shaped((8, 768, PIECE), low),
        shaped((2, 3072, PIECE), low),
        shaped((8, 1, PIECE)),
        shaped((8, 768)),
    )
    scratch = [
        pltpu.VMEM((8, 256, PIECE), low),
        pltpu.VMEM((8, 256, PIECE), jnp.float32),
        pltpu.VMEM((256, 768), low),
        pltpu.VMEM((256, 768), jnp.float32),
        pltpu.VMEM((768, 256), low),
    ]
    args = (a2, x1, att, dy, modulation, expand, lower, biases)
    return call_kernel(perceptron_kernel, outs, args, scratch, 7200000000)


def attention_backward(datt, qkv, lse, o, a1, weight):
    low = jnp.bfloat16
    outs = (shaped((256, 2304), low), shaped((8, 768, PIECE), low))
    return call_kernel(
        attention_backward_kernel,
        outs,
        (datt, qkv, lse, o, a1, weight),
        [pltpu.VMEM((256, 768), low)],
        2500000000,
    )


def input_backward(*args):
    outs = (shaped((256, 768)), shaped((1, VECTOR)))
    return call_kernel(input_backward_kernel, outs, args, [], 900000000)


def update(*args):
    outs = tuple(shaped(shape) for shape in 4 * [(BLOCK, 10752)] + 4 * [(96, 768)])
    return call_kernel(update_kernel, outs, args, [], 10000000)


def adamw(weight, first_mom, second_mom, gradient, decay):
    new_first = beta_one * first_mom + (1.0 - beta_one) * gradient
    new_second = beta_two * second_mom + (1.0 - beta_two) * gradient * gradient
    update = new_first / correct_one / (jnp.sqrt(new_second / correct_two) + adam_eps)
    return (weight - learn_rate * (update + decay * weight), new_first, new_second)

def index_of(x, y, z, core):
    return (y * 2 + x % 2) * 32 + z * 4 + (x // 2) * 2 + core


def pairs_of(move):
    pairs = []
    for x in range(4):
        for y in range(4):
            for z in range(8):
                for core in range(2):
                    there = move(x, y, z, core)
                    pairs.append((index_of(x, y, z, core), index_of(*there)))
    return pairs


MOVES = {
    "c": pairs_of(lambda x, y, z, core: (x, y, z, 1 - core)),
    "xh": pairs_of(lambda x, y, z, core: (3 - x, y, z, core)),
    "xl": pairs_of(lambda x, y, z, core: (x ^ 1, y, z, core)),
    "y0": pairs_of(lambda x, y, z, core: (x, y ^ 1, z, core)),
    "y1": pairs_of(lambda x, y, z, core: (x, 3 - y, z, core)),
    "z0": pairs_of(lambda x, y, z, core: (x, y, z ^ 1, core)),
    "z1": pairs_of(lambda x, y, z, core: (x, y, z ^ 2, core)),
    "z2": pairs_of(lambda x, y, z, core: (x, y, z ^ 4, core)),
    "x+": pairs_of(lambda x, y, z, core: ((x + 1) % 4, y, z, core)),
    "x-": pairs_of(lambda x, y, z, core: ((x + 3) % 4, y, z, core)),
    "y+": pairs_of(lambda x, y, z, core: (x, (y + 1) % 4, z, core)),
    "x2": pairs_of(lambda x, y, z, core: (x ^ 2, y, z, core)),
    "y2": pairs_of(lambda x, y, z, core: (x, y ^ 2, z, core)),
    "y-": pairs_of(lambda x, y, z, core: (x, (y + 3) % 4, z, core)),
}
BLOCK = 24
PIECE = 384


def place(rep, shard):
    y, xl = rep >> 1, rep & 1
    z, xh, c = shard >> 2, (shard >> 1) & 1, shard & 1
    return {
        "z2": z >> 2,
        "z1": (z >> 1) & 1,
        "z0": z & 1,
        "xh": xh,
        "c": c,
        "xl": xl,
        "y0": y & 1,
        "y1": y >> 1,
        "x": xh * 2 + xl,
        "y": y,
    }


def swap(values, move):
    return lax.ppermute(values, ("rep", "shard"), MOVES[move])


def tie(*values):
    return lax.optimization_barrier(values)


def join(mine, theirs, here, axis):
    low = jnp.where(here == 0, mine, theirs)
    high = jnp.where(here == 0, theirs, mine)
    return jnp.concatenate([low, high], axis=axis)


def gather(values, bit, here, axis):
    return join(values, swap(values, bit), here[bit], axis)


def take_half(values, which, axis):
    half = values.shape[axis] // 2
    return lax.dynamic_slice_in_dim(values, which * half, half, axis)


def add_up(*terms):
    total = terms[0].astype(jnp.float32)
    for term in terms[1:]:
        total = total + term.astype(jnp.float32)
    return total.astype(terms[0].dtype)


def scatter(values, bit, here, axis):
    sent = take_half(values, 1 - here[bit], axis)
    kept = take_half(values, here[bit], axis)
    return add_up(kept, swap(sent, bit))


def assemble_kernel(*refs):
    inputs, (first, second, down), sems = refs[:20], refs[20:23], refs[23]
    rep, shard = lax.axis_index("rep"), lax.axis_index("shard")
    y, x = rep // 2, ((shard // 2) % 2) * 2 + rep % 2
    c = shard % 2
    steps = (0, 1, 3, 2, 2)
    for stream in range(2):
        for side in range(2):
            core = c if side == 0 else 1 - c
            for kind in range(5):
                ref = inputs[(stream * 2 + side) * 5 + kind]
                z_start = 4 * stream + (2 if kind == 4 else 0)
                z_count = 2 if kind >= 3 else 4
                for other in range(4):
                    ahead, inner = steps[kind], (0, 1, 2, 3)[other]
                    x_at = (x + (inner if stream == 0 else ahead)) % 4
                    y_at = (y + (ahead if stream == 0 else inner)) % 4
                    xh, xl = x_at // 2, x_at % 2
                    zs = pl.ds(z_start, z_count)
                    for part in range(3):
                        if part == 2:
                            target = down.at[xl, zs, xh, core, y_at]
                        else:
                            target = (first, second)[part].at[y_at, xl, zs, xh, core]
                        pltpu.make_async_copy(ref.at[other, part], target, sems.at[part]).start()
    for part, out in enumerate((first, second, down)):
        pltpu.make_async_copy(out, out, sems.at[part]).wait()


def assemble(pieces):
    shape = jax.ShapeDtypeStruct((4, 2, 8, 2, 2, BLOCK, PIECE), jnp.bfloat16)
    down = jax.ShapeDtypeStruct((2, 8, 2, 2, 4, BLOCK, PIECE), jnp.bfloat16)
    return pl.pallas_call(
        assemble_kernel,
        out_shape=(shape, shape, down),
        in_specs=[pl.BlockSpec(memory_space=pl.ANY)] * 20,
        out_specs=[pl.BlockSpec(memory_space=pltpu.VMEM)] * 3,
        scratch_shapes=[pltpu.SemaphoreType.DMA((3,))],
        compiler_params=pltpu.CompilerParams(vmem_limit_bytes=48 * 1024 * 1024),
        cost_estimate=pl.CostEstimate(flops=0, bytes_accessed=30000000, transcendentals=0),
    )(*pieces)


def own_pieces(rows_weight, down_weight, rep):
    return jnp.stack(
        [
            lax.dynamic_slice(rows_weight, (0, 4608 + PIECE * rep), (BLOCK, PIECE)),
            lax.dynamic_slice(rows_weight, (0, 7680 + PIECE * rep), (BLOCK, PIECE)),
            lax.dynamic_slice(
                down_weight, (BLOCK * (rep >> 1), PIECE * (rep & 1)), (BLOCK, PIECE)
            ),
        ]
    ).astype(jnp.bfloat16)


def ring_round_one(block, axis):
    return swap(block, axis + "+"), swap(block, axis + "-")


def ring_round_two(before, after, axis, cut_axis):
    half = before.shape[cut_axis] // 2
    low = lax.slice_in_dim(before, 0, half, axis=cut_axis)
    high = lax.slice_in_dim(after, half, 2 * half, axis=cut_axis)
    return swap(low, axis + "+"), swap(high, axis + "-")


def gather_weights(values, small, partial_of, here):
    blocks = [values[4 * k : 4 * k + 4].transpose(1, 0, 2, 3)[None] for k in range(2)]
    first_axes, last_axes = ("x", "y"), ("y", "x")
    direct = [[swap(blocks[k], first_axes[k] + step) for step in ("-", "2", "+")] for k in range(2)]
    direct, small = tie(direct, small)
    blocks = [
        jnp.concatenate([blocks[k]] + direct[k], axis=0) for k in range(2)
    ]
    near = [ring_round_one(blocks[k], last_axes[k]) for k in range(2)]
    partial = partial_of(small)
    biases = gather(gather(small, "xh", here, 3), "c", here, 4)
    partial = scatter(partial, "z0", here, 2)
    near, partial, biases = tie(near, partial, biases)
    far = [ring_round_two(*near[k], last_axes[k], 2) for k in range(2)]
    for bit, axis in (("z1", 1), ("z2", 0)):
        partial = scatter(partial, bit, here, axis)
    pieces = []
    for k in range(2):
        mine = [blocks[k], near[k][1], near[k][0], far[k][0], far[k][1]]
        pieces += mine + [swap(piece, "c") for piece in mine]
    biases = biases.reshape(32, -1)[:, :360].reshape(1, -1)
    return assemble(pieces), partial.reshape(1, -1), biases


ROWS_SHAPE = (4, 2, 8, 2, 2, BLOCK, PIECE)
DOWN_SHAPE = (2, 8, 2, 2, 4, BLOCK, PIECE)


def core_swap(gradient, shape, here):
    gradient = gradient.reshape(shape)
    axis = 4 if shape is ROWS_SHAPE else 3
    sent = lax.dynamic_index_in_dim(gradient, 1 - here["c"], axis, keepdims=True)
    return gradient, swap(sent, "c"), shape


def place_block(part, axis, which, zs, here):
    whole, received, shape = part
    first, count = zs
    xh, xl = which // 2, which % 2
    found = []
    for values, core in ((whole, here["c"]), (received, 0)):
        if axis == "x":
            if shape is ROWS_SHAPE:
                start, size = (0, xl, first, xh, core, 0, 0), (4, 1, count, 1, 1, BLOCK, PIECE)
            else:
                start, size = (xl, first, xh, core, 0, 0, 0), (1, count, 1, 1, 4, BLOCK, PIECE)
        elif shape is ROWS_SHAPE:
            start, size = (which, 0, first, 0, core, 0, 0), (1, 2, count, 2, 1, BLOCK, PIECE)
        else:
            start, size = (0, first, 0, core, which, 0, 0), (2, count, 2, 1, 1, BLOCK, PIECE)
        block = lax.dynamic_slice(values, start, size)
        if axis == "x" and shape is ROWS_SHAPE:
            block = block.reshape(4, count, BLOCK, PIECE)
        elif axis == "x":
            block = block.reshape(count, 4, BLOCK, PIECE).transpose(1, 0, 2, 3)
        else:
            block = block.reshape(2, count, 2, BLOCK, PIECE).transpose(2, 0, 1, 3, 4)
            block = block.reshape(4, count, BLOCK, PIECE)
        found.append(block)
    return found


def stacked(parts, axis, steps, zs, here, passed=()):
    which = (here[axis] + steps) % 4
    sums = []
    for number, part in enumerate(parts):
        terms = place_block(part, axis, which, zs, here) + [one[number] for one in passed]
        sums.append(add_up(*terms))
    return jnp.stack(sums)


def scatter_places(parts, vectors, here):
    axes = (("x", "y"), ("y", "x"))
    passed = []
    for k in range(2):
        axis = axes[k][0]
        low = stacked(parts, axis, 2, (4 * k, 2), here)
        high = stacked(parts, axis, 2, (4 * k + 2, 2), here)
        passed.append((swap(low, axis + "+"), swap(high, axis + "-")))
    vectors = gather(vectors, "z2", here, 0)
    *passed, vectors = tie(*passed, vectors)
    vectors = gather(vectors, "z1", here, 1)
    streams = []
    for k in range(2):
        axis = axes[k][0]
        low, high = passed[k]
        halves = ((4 * k, 2), (4 * k + 2, 2))
        ahead = jnp.concatenate(
            [
                stacked(parts, axis, 1, halves[0], here, (low,)),
                stacked(parts, axis, 1, halves[1], here),
            ],
            axis=2,
        )
        back = jnp.concatenate(
            [
                stacked(parts, axis, 3, halves[0], here),
                stacked(parts, axis, 3, halves[1], here, (high,)),
            ],
            axis=2,
        )
        got = (swap(ahead, axis + "+"), swap(back, axis + "-"))
        streams.append(stacked(parts, axis, 0, (4 * k, 4), here, got))
    sent = []
    for k in range(2):
        axis = axes[k][1]
        for step, move in ((1, "+"), (3, "-"), (2, "2")):
            value = lax.dynamic_index_in_dim(
                streams[k], (here[axis] + step) % 4, 1, keepdims=False
            )
            sent.append((value, axis + move))
    *values, vectors = tie(*[value for value, _ in sent], vectors)
    vectors = gather(vectors, "z0", here, 2)
    got = [swap(value, move) for value, (_, move) in zip(values, sent)]
    *got, vectors = tie(*got, vectors)
    results = []
    for k in range(2):
        mine = lax.dynamic_index_in_dim(streams[k], here[axes[k][1]], 1, keepdims=False)
        results.append(add_up(mine, *got[3 * k : 3 * k + 3]))
    return jnp.concatenate(results, axis=1), vectors


def gather_pieces(values, here):
    number = values.shape[0]
    values = values.reshape(1, 1, number, BLOCK, PIECE)
    values = gather(values, "xl", here, 1)
    before, after, far = swap(values, "y+"), swap(values, "y-"), swap(values, "y2")
    return jnp.concatenate([values, after, far, before], axis=0).astype(jnp.float32)


def condition(steps, classes, class_table, first, count):
    half_width = class_table.shape[1] // 2
    column = first + jnp.arange(count)
    place_of = jnp.where(column < half_width, column, column - half_width)
    frequency = jnp.exp(-math.log(10000.0) * place_of.astype(jnp.float32) / half_width)
    angles = steps.astype(jnp.float32)[:, None] * frequency[None, :]
    time_embed = jnp.where(column[None, :] < half_width, jnp.cos(angles), jnp.sin(angles))
    label_rows = jnp.take(class_table, classes, axis=0)
    label_part = lax.dynamic_slice(label_rows, (0, first), (label_rows.shape[0], count))
    return jax.nn.silu(time_embed + label_part.astype(jnp.float32)).astype(jnp.bfloat16)


def local(
    latents,
    cotangent,
    step_ids,
    class_ids,
    class_table,
    rows_weight,
    down_weight,
    bias_weight,
    rows_first,
    down_first,
    bias_first,
    rows_second,
    down_second,
    bias_second,
):
    rep, shard = lax.axis_index("rep"), lax.axis_index("shard")
    here = place(rep, shard)
    width = latents.shape[-1]
    small = jnp.concatenate(
        [
            bias_weight.astype(jnp.bfloat16).astype(jnp.float32),
            step_ids.astype(jnp.float32),
            class_ids.astype(jnp.float32),
            jnp.zeros((22,), jnp.float32),
        ]
    ).reshape(1, 1, 1, 1, 1, -1)
    ada_rows = rows_weight[:, : 6 * width].astype(jnp.bfloat16).reshape(1, 1, BLOCK, 6 * width)
    blocks = own_pieces(rows_weight, down_weight, rep).reshape(1, 1, 1, 3, BLOCK, PIECE)
    ada_rows = gather(ada_rows, "xh", here, 0)
    for axis, bit in ((0, "z2"), (1, "z1"), (2, "z0")):
        blocks, small = tie(blocks, small)
        blocks, small = gather(blocks, bit, here, axis), gather(small, bit, here, axis)
        if bit == "z1":
            ada_rows = gather(ada_rows, "c", here, 1)
    blocks, small, ada_rows = tie(blocks, small, ada_rows)

    def partial_of(small):
        small = small.reshape(8, -1)
        classes = small[:, 361].astype(jnp.int32)
        columns = condition(small[:, 360], classes, class_table, 96 * (shard // 4), 96)
        partial = jnp.dot(
            columns, ada_rows.reshape(96, 6 * width), preferred_element_type=jnp.float32
        )
        return partial.reshape(2, 2, 2, 1, 1, -1)

    (first, second, lower), modulation, biases = gather_weights(
        blocks.reshape(8, 3, BLOCK, PIECE), small, partial_of, here
    )
    first, second = first.reshape(8, 768, PIECE), second.reshape(8, 768, PIECE)
    lower = lower.reshape(2, 3072, PIECE)
    cond_act = condition(step_ids, class_ids, class_table, 0, width).astype(jnp.float32)
    x, dy = latents[0], cotangent[0]
    a1, qkv, lse, o, att, x1, a2 = attention_forward(x, modulation, biases, first)
    output, dx1, datt, expand_grad, lower_grad, hidden_sum, sums = perceptron(
        a2, x1, att, dy, modulation, second, lower, biases
    )
    early = [
        core_swap(expand_grad, ROWS_SHAPE, here)[:2],
        core_swap(lower_grad, DOWN_SHAPE, here)[:2],
    ]
    dqkv, first_grad = attention_backward(datt, qkv, lse, o, a1, first)
    dx, vector = input_backward(
        dqkv, x, dx1, modulation, biases, first, sums, hidden_sum, cond_act
    )
    early, first_grad, dx, vector = tie(early, first_grad, dx, vector)
    parts = [core_swap(first_grad, ROWS_SHAPE, here)]
    parts.append((*early[0], ROWS_SHAPE))
    parts.append((*early[1], DOWN_SHAPE))
    output, grad_latents = output[None], dx[None]
    vectors = vector.astype(jnp.bfloat16).reshape(1, 1, 1, 1, 1, -1)

    def ada_part(vectors):
        vectors = vectors.reshape(32, -1)
        dmod = vectors[:, : 6 * width]
        columns = lax.dynamic_slice(vectors, (0, 15 * width + BLOCK * shard), (32, BLOCK))
        ada_term = dot_of(columns, dmod, 0, 0)
        bias_sum = jnp.sum(vectors[:, : 15 * width].astype(jnp.float32), axis=0)
        bias_sum = lax.dynamic_slice(bias_sum, (360 * shard,), (360,))
        bias_sum = jnp.pad(bias_sum, (0, 24)).reshape(3, 128).repeat(8, axis=0)
        return jnp.concatenate([ada_term, bias_sum], axis=1).astype(jnp.bfloat16)

    owned, vectors = scatter_places(parts, vectors, here)
    owned = owned.reshape(3, 2, 2, 2, BLOCK, PIECE)
    owned = scatter(owned, "z0", here, 3)
    vectors = gather(vectors, "xh", here, 3)
    owned, vectors = tie(owned, vectors)
    owned = scatter(owned, "z1", here, 2)
    packed = ada_part(gather(vectors, "c", here, 4))
    owned, packed = tie(owned, packed)
    owned = scatter(owned, "z2", here, 1).reshape(3, BLOCK, PIECE)
    packed = add_up(packed, swap(packed, "xl"))
    owned, packed = tie(owned, packed)
    for bit in ("y0", "y1"):
        packed = add_up(packed, swap(packed, bit))
    packed = packed.astype(jnp.float32)
    owned = gather_pieces(owned, here)
    (
        grad_rows,
        new_rows,
        first_rows,
        second_rows,
        grad_down,
        new_down,
        first_down,
        second_down,
    ) = update(
        packed,
        owned,
        rows_weight,
        rows_first,
        rows_second,
        down_weight,
        down_first,
        down_second,
    )
    grad_bias = packed[::8, 6 * width :].reshape(-1)[:360] * (1.0 / 65536)
    new_bias, first_bias, second_bias = adamw(bias_weight, bias_first, bias_second, grad_bias, 0.0)
    return (
        output,
        grad_latents,
        grad_rows,
        grad_down,
        grad_bias,
        new_rows,
        new_down,
        new_bias,
        first_rows,
        first_down,
        first_bias,
        second_rows,
        second_down,
        second_bias,
    )


def solution(mesh):
    placed = (
        P(("rep", "shard"), None, None),
        P(("rep", "shard"), None, None),
        P(("rep", "shard")),
        P(("rep", "shard")),
        P(),
        P("shard", None),
        P("shard", None),
        P("shard"),
        P("shard", None),
        P("shard", None),
        P("shard"),
        P("shard", None),
        P("shard", None),
        P("shard"),
    )
    return jax.shard_map(
        local,
        mesh=mesh,
        in_specs=placed,
        out_specs=(
            P(("rep", "shard"), None, None),
            P(("rep", "shard"), None, None),
            P("shard", None),
            P("shard", None),
            P("shard"),
            P("shard", None),
            P("shard", None),
            P("shard"),
            P("shard", None),
            P("shard", None),
            P("shard"),
            P("shard", None),
            P("shard", None),
            P("shard"),
        ),
        check_vma=False,
    )
```
